32 devices in a mesh: img: 8 (over z, x), seq: 4 (over y, core).
Axes of the slice: x: 2, y: 2, z: 4, core: 2. Of those that a mesh axis runs over, the one named last changes fastest.
Arguments:
- media_tokens: bfloat16 [16, 576, 1024], P('img', 'seq'), may hold values from -6 to 6
- latents: bfloat16 [16, 64, 1024], P('img', 'seq'), may hold values from -6 to 6
- patch_count: int32 [16], P('img'), may hold values from 256 to 576, as said below
- w_query: bfloat16 [2, 1024, 512], P(None, ('img', 'seq')), may hold values from -0.1875 to 0.1875
- w_keyval: bfloat16 [2, 1024, 1024], P(None, ('img', 'seq')), may hold values from -0.1875 to 0.1875
- w_out: bfloat16 [2, 512, 1024], P(None, ('img', 'seq')), may hold values from -1 to 1
- w_up: bfloat16 [2, 1024, 4096], P(None, ('img', 'seq')), may hold values from -0.1875 to 0.1875
- w_down: bfloat16 [2, 4096, 1024], P(None, ('img', 'seq')), may hold values from -0.09375 to 0.09375
- norm_params: bfloat16 [2, 6, 1024], P(None, None, ('img', 'seq')), may hold values from -1.2 to 1.4, as said below
- cotangent: bfloat16 [16, 64, 1024], P('img', 'seq'), may hold values from -6 to 6
Outputs:
- latents_out: bfloat16 [16, 64, 1024], P('img', 'seq')
- grad_media: float32 [16, 576, 1024], P('img', 'seq')
- grad_latents: float32 [16, 64, 1024], P('img', 'seq')
- grad_query: float32 [2, 1024, 512], P(None, ('img', 'seq'))
- grad_keyval: float32 [2, 1024, 1024], P(None, ('img', 'seq'))
- grad_outproj: float32 [2, 512, 1024], P(None, ('img', 'seq'))
- grad_up: float32 [2, 1024, 4096], P(None, ('img', 'seq'))
- grad_down: float32 [2, 4096, 1024], P(None, ('img', 'seq'))
- grad_norms: float32 [2, 6, 1024], P(None, None, ('img', 'seq'))
The draws below stay inside these ranges and needn't reach their ends.
Inputs may be any that keep to these rules, and one draw needn't show every extreme that they name: `patch_count`: each image has 256 or 576 live patches, the first ones of its slots; the images with 576 form one run of consecutive image numbers, wrapping around from the last to the first; some image has 576 and some 256. `norm_params`: gains in rows 0, 2 and 4, shifts in rows 1, 3 and 5.
All inputs are finite; a program needn't handle non-finite values.
Results may differ from the reference program's by a relative error of at most 0.025.
Values may be sent and summed in bfloat16 or wider, within the bound.
A program may use at most 192 MiB of HBM per device.

```python
import jax
import jax.numpy as jnp
from jax import lax

D = 1024
HEAD = 64
FF = 4096
LATENTS = 64
LAYERS = 2
PATCH_BIG = 576
PATCH_SMALL = 256
INNER = 512
IMAGES = 16


def draw_patch_count(key, part):
    key = jax.random.fold_in(key, 11)
    key_one, key_two = jax.random.split(key)
    count_big = jax.random.randint(key_one, (), 1, IMAGES)
    start = jax.random.randint(key_two, (), 0, IMAGES)
    offset = (jnp.arange(IMAGES, dtype=jnp.int32) - start) % IMAGES
    return jnp.where(offset < count_big, PATCH_BIG, PATCH_SMALL).astype(jnp.int32)


def draw_norm_params(key, part):
    key = jax.random.fold_in(key, 5)
    key_one, key_two = jax.random.split(key)
    gains = jax.random.uniform(key_one, (LAYERS, 6, D), jnp.float32, 0.6, 1.4)
    shifts = jnp.clip(0.3 * jax.random.normal(key_two, (LAYERS, 6, D), jnp.float32), -1.2, 1.2)
    row_kind = jnp.arange(6)[None, :, None] % 2
    return jnp.where(row_kind == 0, gains, shifts).astype(jnp.bfloat16)


def block_scale(own_key, dims, pieces, low, high):
    level, own = 1.0, jax.random.fold_in(own_key, 6)
    for axis_at, shards_of in pieces:
        draws = jnp.exp(jax.random.uniform(jax.random.fold_in(own, axis_at), (shards_of,), jnp.float32, low / len(pieces), high / len(pieces)))
        level = level * jnp.repeat(draws, dims[axis_at] // shards_of).reshape([-1 if axis == axis_at else 1 for axis in range(len(dims))])
    return level


def normal_values(stream_key, dims, scale, bound, cuts=(), kind=jnp.bfloat16):
    factor_of = block_scale(stream_key, dims, cuts, -0.22, 0.18) if cuts else 1.0
    array = jax.random.normal(stream_key, dims, jnp.float32) * scale * factor_of
    return jnp.minimum(jnp.maximum(array, -bound), bound).astype(kind)


def setup_inputs(seed: int = 0) -> dict:
    streams_of = jax.random.split(jax.random.key(seed), 11)
    media_tokens = normal_values(streams_of[0], (IMAGES, PATCH_BIG, D), 1.0, 6.0, ((0, 8), (1, 4)))
    latents = normal_values(streams_of[1], (IMAGES, LATENTS, D), 1.0, 6.0, ((0, 8), (1, 4)))
    patch_count = draw_patch_count(jax.random.fold_in(streams_of[10], 71), 0)
    w_query = normal_values(streams_of[3], (LAYERS, D, INNER), D ** -0.5, 0.1875, ((1, 32),))
    w_keyval = normal_values(streams_of[4], (LAYERS, D, 2 * INNER), D ** -0.5, 0.1875, ((1, 32),))
    w_out = normal_values(streams_of[5], (LAYERS, INNER, D), 32 ** -0.5, 1.0, ((1, 32),))
    w_up = normal_values(streams_of[6], (LAYERS, D, FF), D ** -0.5, 0.1875, ((1, 32),))
    w_down = normal_values(streams_of[7], (LAYERS, FF, D), FF ** -0.5, 0.09375, ((1, 32),))
    norm_params = draw_norm_params(jax.random.fold_in(streams_of[10], 71), 0)
    cotangent = normal_values(streams_of[9], (IMAGES, LATENTS, D), 1.0, 6.0, ((0, 8), (1, 4)))
    return dict(media_tokens=media_tokens, latents=latents, patch_count=patch_count, w_query=w_query, w_keyval=w_keyval, w_out=w_out, w_up=w_up, w_down=w_down, norm_params=norm_params, cotangent=cotangent)


@jax.custom_vjp
def low(v):
    return lax.optimization_barrier(v.astype(jnp.bfloat16)).astype(jnp.float32)

@jax.custom_vjp
def low_back(v):
    return v

def low_keep(v):
    return (low(v), None)

def low_pass(kept, grad):
    return (grad,)

def back_keep(v):
    return (v, None)

def back_low(kept, grad):
    return (low(grad),)
low.defvjp(low_keep, low_pass)
low_back.defvjp(back_keep, back_low)
highest = lax.Precision.HIGHEST
eps = 1e-05

def norm_rows(values, gain, shift):
    centre = lax.optimization_barrier(jnp.mean(values, axis=-1, keepdims=True))
    centred = values - centre
    spread = lax.optimization_barrier(jnp.mean(centred * centred, axis=-1, keepdims=True))
    return centred * lax.rsqrt(spread + eps) * gain + shift

def matmul(left, right):
    return jnp.matmul(left, right, precision=highest)

def attend_image(packed):
    query_rows, media_kv, latent_kv, live_media = packed
    inner_width = query_rows.shape[1]
    keys_all = jnp.concatenate([media_kv, latent_kv], axis=0)
    query_heads = query_rows.reshape(query_rows.shape[0], -1, HEAD)
    key_heads = keys_all[:, :inner_width].reshape(keys_all.shape[0], -1, HEAD)
    value_heads = keys_all[:, inner_width:].reshape(keys_all.shape[0], -1, HEAD)
    scores = low_back(jnp.einsum('lhd,khd->hlk', query_heads, key_heads, precision=highest) * 0.125)
    live_keys = jnp.concatenate([live_media, jnp.ones((latent_kv.shape[0],), dtype=jnp.bool_)], axis=0)
    scores = jnp.where(live_keys[None, None, :], scores, -1000000000.0)
    row_top = lax.optimization_barrier(jnp.max(scores, axis=-1, keepdims=True))
    expo = jnp.exp(scores - row_top)
    row_total = lax.optimization_barrier(jnp.sum(expo, axis=-1, keepdims=True))
    mixed_heads = jnp.einsum('hlk,khd->hld', low(expo), value_heads, precision=highest) / row_total
    return jnp.transpose(mixed_heads, (1, 0, 2)).reshape(query_rows.shape[0], inner_width)

def forward(media_float, latent_float, w_query, w_keyval, w_out, w_up, w_down, norm_params, live_media):
    current = latent_float
    for layer_id in range(LAYERS):
        normed = norm_params[layer_id]
        media_normed = low(norm_rows(media_float, normed[0], normed[1]))
        media_kv = low(low_back(matmul(media_normed, w_keyval[layer_id])))
        latent_normed = low(norm_rows(current, normed[2], normed[3]))
        queries = low(low_back(matmul(latent_normed, w_query[layer_id])))
        latent_kv = low(low_back(matmul(latent_normed, w_keyval[layer_id])))
        attended = lax.map(jax.checkpoint(attend_image), (queries, media_kv, latent_kv, live_media))
        attended = low(low_back(attended))
        after_attn = current + low_back(matmul(attended, w_out[layer_id]))
        ff_normed = low(norm_rows(after_attn, normed[4], normed[5]))
        hidden_pre = low_back(matmul(ff_normed, w_up[layer_id]))
        activated = low(jax.nn.gelu(hidden_pre, approximate=False))
        current = after_attn + low_back(matmul(activated, w_down[layer_id]))
    return current

def reference(media_tokens, latents, patch_count, w_query, w_keyval, w_out, w_up, w_down, norm_params, cotangent):
    positions = jnp.arange(PATCH_BIG).astype(jnp.int32)
    live_media = positions[None, :] < patch_count.astype(jnp.int32)[:, None]

    def closed(media_float, latent_float, query_w, keyval_w, out_w, up_w, down_w, norm_w):
        return forward(media_float, latent_float, query_w, keyval_w, out_w, up_w, down_w, norm_w, live_media)
    result, pullback = jax.vjp(closed, media_tokens.astype(jnp.float32), latents.astype(jnp.float32), w_query.astype(jnp.float32), w_keyval.astype(jnp.float32), w_out.astype(jnp.float32), w_up.astype(jnp.float32), w_down.astype(jnp.float32), norm_params.astype(jnp.float32))
    grads = pullback(cotangent.astype(jnp.float32))
    return (result.astype(jnp.bfloat16), grads[0], grads[1], grads[2], grads[3], grads[4], grads[5], grads[6], grads[7])
```

```python
import functools

import jax
import jax.numpy as jnp
from jax import lax
from jax.experimental import pallas as pl
from jax.experimental.pallas import tpu as pltpu
from jax.sharding import PartitionSpec as P

HEAD = 64
EPS = 1e-05
MESH = pl.DeviceIdType.MESH
BF = jnp.bfloat16
F32 = jnp.float32
TP = 8


class Sizes:
    def __init__(self, mesh, media, latents, wq, wkv, wout, wup, wdown):
        self.ni, self.ns = mesh.shape["img"], mesh.shape["seq"]
        self.ny = self.ns // 2
        self.chips = self.ni * self.ny
        self.layers = wq.shape[0]
        self.d = media.shape[2]
        self.nimg, self.pr = media.shape[0], media.shape[1]
        self.lr = latents.shape[1]
        self.inner = wq.shape[2]
        self.half = self.inner // 2
        self.ff = wup.shape[2]
        self.fs = self.ff // TP
        self.dp = self.chips // TP
        self.fc = self.ff // self.chips
        self.pm = self.pr * self.ns
        self.latn = self.lr * self.ns
        self.r = self.latn // 2
        self.keys = self.pm + self.latn
        self.heads = self.half // HEAD
        self.rows = TP * self.r
        self.mt = BF if self.pr % 16 == 0 else F32
        self.lt = BF if self.lr % 16 == 0 else F32
        assert self.nimg == self.ny and TP % self.ny == 0


def dot(a, b, ca=1, cb=0):
    return lax.dot_general(a, b, (((ca,), (cb,)), ((), ())), preferred_element_type=F32)


def centre(v):
    c = v - jnp.mean(v, axis=-1, keepdims=True)
    rstd = lax.rsqrt(jnp.mean(c * c, axis=-1, keepdims=True) + EPS)
    return c * rstd, rstd


def pull(xhat, rstd, cot, gain):
    g = cot * gain
    m1 = jnp.mean(g, axis=-1, keepdims=True)
    m2 = jnp.mean(g * xhat, axis=-1, keepdims=True)
    return rstd * (g - m1 - xhat * m2)


def col_sum(v):
    return jnp.sum(v, axis=0, keepdims=True)


def kernel(z, media_in, latcot_in, counts, nrm_in, wqkv_in, wo_in, wup_in, wdn_in,
           lat_out, gmedia_out, glat_out, gqkv, gout, gup, gdn, gn_out,
           media, lc, mn, kv, wqkv, wo, wup, wdn, nrm, q4, pexp, rtot, att4, atta, aft,
           ffa, hp, act, xs, gza, psend, precv, gpre, gya, gl, grecv, gkvm, macc, msend, mrecv, gn, xout, gxo, cm, fold,
           ss, rs, ls):
    L = z.layers
    i = lax.axis_index("img")
    s = lax.axis_index("seq")
    y, c = s // 2, s % 2
    k = i * z.ny + y
    pos, grp = k % TP, k // TP
    sib = (i, y * 2 + (1 - c))

    def chip(kk, cc):
        return (kk // z.ny, (kk % z.ny) * 2 + cc)

    def peer(t):
        return chip(grp * TP + (pos + t) % TP, c)

    waits = []
    count = [0]

    def sem():
        count[0] += 1
        return count[0] - 1

    def send(src, dst, dev, n):
        pltpu.make_async_remote_copy(src, dst, ss.at[n], rs.at[n], device_id=dev, device_id_type=MESH).start()

    def arrive(ref, n):
        pltpu.make_async_copy(ref, ref, rs.at[n]).wait()

    def local(src, dst, n):
        pltpu.make_async_copy(src, dst, ls.at[n]).start()

    def landed(src, dst, n):
        pltpu.make_async_copy(src, dst, ls.at[n]).wait()

    def sent(ref, n):
        waits.append((ref, n))

    bar = pltpu.get_barrier_semaphore()
    total = z.ni * z.ns
    me = i * z.ns + s

    def greet(t, _):
        o = (me + t) % total
        pl.semaphore_signal(bar, inc=1, device_id=(o // z.ns, o % z.ns), device_id_type=MESH)
        return 0

    lax.fori_loop(1, total, greet, 0)
    pl.semaphore_wait(bar, total - 1)

    loads = [(nrm_in, nrm), (wqkv_in.at[0], wqkv.at[0]), (wo_in.at[0], wo.at[0]), (wup_in.at[0], wup.at[0]),
             (wdn_in.at[0], wdn.at[0]), (wqkv_in.at[1], wqkv.at[1]), (wo_in.at[1], wo.at[1]),
             (wup_in.at[1], wup.at[1]), (wdn_in.at[1], wdn.at[1])]

    n_lc, n_ma, n_mb = sem(), sem(), sem()
    own_slot = s % z.ny
    for yy in range(z.ny):
        to = yy * 2 + s // z.ny

        @pl.when(to != s)
        def _():
            send(latcot_in.at[yy], lc.at[own_slot], (i, to), n_lc)

        @pl.when(to == s)
        def _():
            pltpu.make_async_copy(latcot_in.at[yy], lc.at[own_slot], rs.at[n_lc]).start()

    for t in range(1, z.ny):
        yy = (y + t) % z.ny
        send(media_in.at[yy], media.at[s], (i, yy * 2 + c), n_ma)
    pltpu.make_async_copy(media_in.at[y], media.at[s], rs.at[n_ma]).start()
    send(media_in.at[y], media.at[s], sib, n_mb)
    for n, (a, b) in enumerate(loads):
        local(a, b, n)
    arrive(lc, n_lc)
    cot = lc[:, 1].astype(F32).reshape(z.r, z.d)
    xs[0] = lc[:, 0].astype(F32).reshape(z.r, z.d)

    n_ff = [sem() for _ in range(L)]
    n_gz = [sem() for _ in range(L)]
    n_rs = [sem() for _ in range(2 * L)]
    n_ln = [sem() for _ in range(L)]
    n_at = [sem() for _ in range(L)]
    n_gy = [sem() for _ in range(L)]
    n_gl = [sem() for _ in range(L)]
    n_md = sem()
    n_lo, n_go, n_mo = sem(), sem(), sem()

    def gather_start(buf, value, n):
        buf[pos] = value
        for t in range(1, TP):
            send(buf.at[pos], buf.at[pos], peer(t), n)

    def gather_end(buf, n):
        arrive(buf.at[pl.ds(0, TP - 1)], n)
        sent(buf.at[pl.ds(0, TP - 1)], n)

    def swap(ref, value, n):
        ref[...] = value
        send(ref, ref, sib, n)
        arrive(ref, n)
        sent(ref, n)

    def pair_swap(buf, value, n):
        swap(buf.at[c], value, n)

    def scatter_sum(part, j):
        n = n_rs[j]
        psend[j] = part.astype(BF).reshape(TP, z.r, z.d)
        for t in range(1, TP):
            o = (pos + t) % TP
            send(psend.at[j, o], precv.at[j, pos], peer(t), n)
        precv[j, pos] = psend[j, pos]

    def scatter_end(j):
        n = n_rs[j]
        arrive(precv.at[j, pl.ds(0, TP - 1)], n)
        sent(precv.at[j, pl.ds(0, TP - 1)], n)
        out = precv[j, 0].astype(F32)
        for t in range(1, TP):
            out = out + precv[j, t].astype(F32)
        return out

    def vec(l, m):
        return nrm[6 * l + m][None, :]

    gather_start(gza.at[L - 1], cot.astype(BF), n_gz[L - 1])

    landed(nrm_in, nrm, 0)
    arrive(media.at[pl.ds(0, z.ny)], n_ma)
    for t in range(1, z.ny):
        yy = (y + t) % z.ny
        send(media.at[yy * 2 + c], media.at[yy * 2 + c], sib, n_mb)
    arrive(media.at[pl.ds(0, z.ny)], n_mb)

    def norm_piece(j, _):
        xhat, rstd = centre(media[j].astype(F32))
        rows = pl.ds(pl.multiple_of(j * z.pr, 8), z.pr)
        for l in range(L):
            mn[l, rows] = (xhat * vec(l, 0) + vec(l, 1)).astype(BF)
        return 0

    lax.fori_loop(0, z.ns, norm_piece, 0)

    lane_head = lax.broadcasted_iota(jnp.int32, (1, z.half), 1) // HEAD

    def stack_heads(v):
        return jnp.concatenate([jnp.where(lane_head == h, v, jnp.zeros_like(v)) for h in range(z.heads)], axis=0)

    def fold_heads(v):
        out = None
        fold[...] = v
        for h in range(z.heads):
            part = jnp.where(lane_head == h, fold[h * z.latn:(h + 1) * z.latn], 0.0)
            out = part if out is None else out + part
        return out

    key_pos = lax.broadcasted_iota(jnp.int32, (1, z.keys), 1)
    live = (key_pos < counts[y]) | (key_pos >= z.pm)

    def media_kv(l):
        kv[l, :z.pm] = dot(mn[l, :z.pm], wqkv[l, :, z.half:]).astype(BF)

    def attention(l):
        xhat, _ = centre(xs[l])
        at = pl.ds(pl.multiple_of(z.pm + c * z.r, 16), z.r)
        swap(mn.at[l, at], (xhat * vec(l, 2) + vec(l, 3)).astype(BF), n_ln[l])
        rows = mn[l, z.pm:]
        qkv = dot(rows, wqkv[l]).astype(BF)
        kv[l, z.pm:] = qkv[:, z.half:]
        q = stack_heads(qkv[:, :z.half])
        q4[l] = q
        scores = dot(q, kv[l, :, :z.half], 1, 1) * 0.125
        scores = jnp.where(live, scores, -1000000000.0)
        e = jnp.exp(scores - jnp.max(scores, axis=-1, keepdims=True))
        rt = jnp.sum(e, axis=-1, keepdims=True)
        pexp[l] = e
        rtot[l] = rt
        mixed = dot(e.astype(BF), kv[l, :, z.half:]) / rt
        own = fold_heads(mixed)
        att4[l] = own
        pair_swap(atta.at[l], own.astype(BF), n_at[l])
        mine = pl.ds(pl.multiple_of(c * z.r, 8), z.r)
        out = dot(jnp.concatenate([atta[l, 0, mine], atta[l, 1, mine]], axis=1), wo[l])
        after = xs[l] + out
        aft[l] = after
        xhat, _ = centre(after)
        gather_start(ffa.at[l], (xhat * vec(l, 4) + vec(l, 5)).astype(BF), n_ff[l])

    def hidden(l):
        gather_end(ffa.at[l], n_ff[l])
        h = dot(ffa[l].reshape(z.rows, z.d), wup[l])
        hp[l] = h
        act[l] = (h * (0.5 * (1.0 + lax.erf(h * 0.7071067811865476)))).astype(BF)

    def down(l):
        scatter_sum(dot(act[l], wdn[l]), l)

    def ff_back(l):
        gather_end(gza.at[l], n_gz[l])
        g = dot(gza[l].reshape(z.rows, z.d), wdn[l], 1, 1)
        h = hp[l]
        slope = 0.5 * (1.0 + lax.erf(h * 0.7071067811865476)) + h * 0.3989422804014327 * jnp.exp(-0.5 * h * h)
        gpre[l] = (g * slope).astype(BF)
        scatter_sum(dot(gpre[l], wup[l], 1, 1), L + l)

    def ff_grads(l):
        gdn[l] = dot(act[l], gza[l].reshape(z.rows, z.d), 0, 0).astype(BF)
        gup[l] = dot(ffa[l].reshape(z.rows, z.d), gpre[l], 0, 0).astype(BF)

    def attn_back(l, gx):
        gff = scatter_end(L + l)
        xhat, rstd = centre(aft[l])
        gn[6 * l + 4] = jnp.sum(gff * xhat, axis=0)
        gn[6 * l + 5] = jnp.sum(gff, axis=0)
        gafter = gx + pull(xhat, rstd, gff, vec(l, 4))
        pair_swap(gya.at[l], gafter.astype(BF), n_gy[l])
        gy = gya[l].reshape(z.latn, z.d)
        wo_own = wo[l, pl.ds(pl.multiple_of(c * z.half, 128), z.half)]
        gatt = dot(gy, wo_own, 1, 1).astype(BF)
        g4 = stack_heads(gatt.astype(F32))
        a4 = stack_heads(att4[l])
        delta = jnp.sum(g4 * a4, axis=-1, keepdims=True)
        rt = rtot[l]
        e = pexp[l]
        gp = dot(g4.astype(BF), kv[l, :, z.half:], 1, 1)
        gs = (e / rt * (gp - delta)).astype(BF)
        gq = (fold_heads(dot(gs, kv[l, :, :z.half])) * 0.125).astype(BF)
        gk = (dot(gs, q4[l], 0, 0) * 0.125).astype(BF)
        gv = dot(e.astype(BF), (g4 / rt).astype(BF), 0, 0).astype(BF)
        glat = jnp.concatenate([gq, gk[z.pm:], gv[z.pm:]], axis=1)
        part = dot(glat, wqkv[l], 1, 1)
        gl[l] = part.reshape(2, z.r, z.d)
        send(gl.at[l, 1 - c], grecv.at[l], sib, n_gl[l])
        gkvm[l, :, :z.half] = gk
        gkvm[l, :, z.half:] = gv
        arrive(grecv.at[l], n_gl[l])
        sent(grecv.at[l], n_gl[l])
        gln = gl[l, c] + grecv[l]
        xhat, rstd = centre(xs[l])
        gn[6 * l + 2] = jnp.sum(gln * xhat, axis=0)
        gn[6 * l + 3] = jnp.sum(gln, axis=0)
        return gafter + pull(xhat, rstd, gln, vec(l, 2)), gq

    def attn_grads(l, gq):
        gqkv[l, :, :z.half] = dot(mn[l, z.pm:], gq, 0, 0).astype(BF)
        gqkv[l, :, z.half:] = dot(mn[l], gkvm[l], 0, 0).astype(BF)
        att = jnp.concatenate([atta[l, 0], atta[l, 1]], axis=1)
        cols = pl.ds(pl.multiple_of(c * (z.d // 2), 128), z.d // 2)
        gyc = jnp.concatenate([gya[l, 0, :, cols], gya[l, 1, :, cols]], axis=0)
        gout[l] = dot(att, gyc, 0, 0).astype(BF)

    def media_back(l):
        cm[...] = dot(gkvm[l, :z.pm], wqkv[l, :, z.half:], 1, 1)

        def piece(j, sums):
            rows = pl.ds(pl.multiple_of(j * z.pr, 8), z.pr)
            xhat, rstd = centre(media[j].astype(F32))
            cotm = cm[rows]
            add = cotm * vec(l, 0)
            macc[rows] = add if l == L - 1 else macc[rows] + add
            return sums[0] + col_sum(cotm * xhat), sums[1] + col_sum(cotm)

        zero = jnp.zeros((1, z.d), F32)
        a, b = lax.fori_loop(0, z.ns, piece, (zero, zero))
        gn[6 * l + 0] = a[0]
        gn[6 * l + 1] = b[0]

    landed(*loads[1], 1)
    media_kv(0)
    landed(*loads[2], 2)
    landed(*loads[3], 3)
    landed(*loads[4], 4)
    for l in range(L):
        attention(l)
        if l == 0:
            for n in range(5, 9):
                landed(*loads[n], n)
            media_kv(1)
        hidden(l)
        if l < L - 1:
            down(l)
            xs[l + 1] = aft[l] + scatter_end(l)
    gx = cot
    for l in reversed(range(L)):
        if l < L - 1:
            gather_start(gza.at[l], gx.astype(BF), n_gz[l])
        ff_back(l)
        if l == L - 1:
            down(l)
        ff_grads(l)
        gx, gq = attn_back(l, gx)
        attn_grads(l, gq)
        media_back(l)
        if l == L - 1:
            xout[...] = (aft[l] + scatter_end(l)).astype(z.lt).reshape(z.ny, z.lr, z.d)
    gxo[...] = gx.reshape(z.ny, z.lr, z.d)

    def give_back(src, out, n):
        for j in range(z.ny):
            to = c * z.ny + j

            @pl.when(to != s)
            def _():
                send(src.at[j], out.at[y], (i, to), n)

            @pl.when(to == s)
            def _():
                pltpu.make_async_copy(src.at[j], out.at[y], rs.at[n]).start()

    give_back(xout, lat_out, n_lo)
    give_back(gxo, glat_out, n_go)
    h = z.pm // 2
    other = pl.ds(pl.multiple_of((1 - c) * h, 8), h)
    mine = pl.ds(pl.multiple_of(c * h, 8), h)
    msend[...] = macc[other].astype(z.mt)
    send(msend, mrecv, sib, n_md)
    arrive(mrecv, n_md)
    sent(mrecv, n_md)
    xhat, rstd = centre(media[pl.ds(c * z.ny, z.ny)].astype(F32).reshape(h, z.d))
    gm = pull(xhat, rstd, macc[mine] + mrecv[...].astype(F32), jnp.ones((1, z.d), F32))
    msend2 = mn.at[0, pl.ds(0, h)]
    if z.mt == BF:
        for j in range(z.ny):
            mn[0, pl.ds(j * z.pr, z.pr)] = gm[j * z.pr:(j + 1) * z.pr].astype(BF)
        srcs = [mn.at[0, pl.ds(j * z.pr, z.pr)] for j in range(z.ny)]
    else:
        macc[:h] = gm
        srcs = [macc.at[pl.ds(j * z.pr, z.pr)] for j in range(z.ny)]
    for j in range(z.ny):
        to = c * z.ny + j

        @pl.when(to != s)
        def _():
            send(srcs[j], gmedia_out.at[y], (i, to), n_mo)

        @pl.when(to == s)
        def _():
            pltpu.make_async_copy(srcs[j], gmedia_out.at[y], rs.at[n_mo]).start()

    gn_out[...] = gn[...]
    arrive(lat_out, n_lo)
    arrive(glat_out, n_go)
    arrive(gmedia_out, n_mo)
    for yy in range(z.ny):
        @pl.when(yy * 2 + s // z.ny != s)
        def _():
            pltpu.make_async_copy(lc.at[0], lc.at[0], ss.at[n_lc]).wait()
    for j in range(z.ny):
        @pl.when(c * z.ny + j != s)
        def _():
            pltpu.make_async_copy(xout.at[0], xout.at[0], ss.at[n_lo]).wait()
            pltpu.make_async_copy(gxo.at[0], gxo.at[0], ss.at[n_go]).wait()
            pltpu.make_async_copy(srcs[0], srcs[0], ss.at[n_mo]).wait()
    if z.ny > 1:
        part = media.at[pl.ds(0, z.ny - 1)]
        pltpu.make_async_copy(part, part, ss.at[n_ma]).wait()
    part = media.at[pl.ds(0, z.ny)]
    pltpu.make_async_copy(part, part, ss.at[n_mb]).wait()
    for ref, n in waits:
        pltpu.make_async_copy(ref, ref, ss.at[n]).wait()


NSEM = 32


def call(z, *args):
    L, D = z.layers, z.d
    V = lambda *shape_dtype: pltpu.VMEM(shape_dtype[:-1], shape_dtype[-1])
    out = lambda *shape_dtype: jax.ShapeDtypeStruct(shape_dtype[:-1], shape_dtype[-1])
    outs = [
        (out(z.ny, z.lr, D, z.lt), pl.ANY),
        (out(z.ny, z.pr, D, z.mt), pl.ANY),
        (out(z.ny, z.lr, D, F32), pl.ANY),
        (out(L, D, 3 * z.half, BF), pltpu.VMEM),
        (out(L, z.inner, D // 2, BF), pltpu.VMEM),
        (out(L, D, z.fs, BF), pltpu.VMEM),
        (out(L, z.fs, D, BF), pltpu.VMEM),
        (out(16, D, F32), pltpu.VMEM),
    ]
    R, T = z.r, TP
    scratch = [
        V(z.ns, z.pr, D, z.mt), V(z.ny, 2, z.lr, D, z.lt), V(L, z.keys, D, BF), V(L, z.keys, 2 * z.half, BF),
        V(L, D, 3 * z.half, BF), V(L, z.inner, D, BF), V(L, D, z.fs, BF), V(L, z.fs, D, BF), V(16, D, F32),
        V(L, z.heads * z.latn, z.half, BF), V(L, z.heads * z.latn, z.keys, F32),
        V(L, z.heads * z.latn, 1, F32), V(L, z.latn, z.half, F32), V(L, 2, z.latn, z.half, BF), V(L, R, D, F32),
        V(L, T, R, D, BF), V(L, z.rows, z.fs, F32), V(L, z.rows, z.fs, BF), V(L, R, D, F32), V(L, T, R, D, BF),
        V(2 * L, T, R, D, BF), V(2 * L, T, R, D, BF), V(L, z.rows, z.fs, BF), V(L, 2, R, D, BF), V(L, 2, R, D, F32),
        V(L, R, D, F32), V(L, z.keys, 2 * z.half, BF), V(z.pm, D, F32), V(z.pm // 2, D, z.mt), V(z.pm // 2, D, z.mt),
        V(16, D, F32), V(z.ny, z.lr, D, z.lt), V(z.ny, z.lr, D, F32), V(z.pm, D, F32), V(z.heads * z.latn, z.half, F32),
        pltpu.SemaphoreType.DMA((NSEM,)), pltpu.SemaphoreType.DMA((NSEM,)), pltpu.SemaphoreType.DMA((16,)),
    ]
    ins = [pl.ANY, pl.ANY, pltpu.SMEM] + [pl.ANY] * 5
    return pl.pallas_call(
        functools.partial(kernel, z),
        out_shape=[o for o, _ in outs],
        in_specs=[pl.BlockSpec(memory_space=m) for m in ins],
        out_specs=[pl.BlockSpec(memory_space=m) for _, m in outs],
        scratch_shapes=scratch,
        compiler_params=pltpu.CompilerParams(collective_id=0, has_side_effects=True, vmem_limit_bytes=60 * 2**20),
    )(*args)


BOTH = ("img", "seq")


def body(mesh, media, latents, counts, wq, wkv, wout, wup, wdown, norms, cotangent):
    z = Sizes(mesh, media, latents, wq, wkv, wout, wup, wdown)
    L, D = z.layers, z.d
    i, s = lax.axis_index("img"), lax.axis_index("seq")
    y, c = s // 2, s % 2
    k = i * z.ny + y
    pos = k % TP

    def pick(a, axis, index):
        return lax.dynamic_index_in_dim(a, index, axis, keepdims=False)

    gather = lambda a, axis: lax.all_gather(a, BOTH, axis=axis, tiled=True)
    nrm = gather(norms, 2).astype(F32).reshape(6 * L, D)
    nrm = jnp.pad(nrm, ((0, 16 - 6 * L), (0, 0)))
    fq = pick(gather(wq, 1).reshape(L, D, 2, z.half), 2, c)
    fkv = pick(gather(wkv, 1).reshape(L, D, 2, 2, z.half), 3, c).reshape(L, D, 2 * z.half)
    wqkv = jnp.concatenate([fq, fkv], axis=2)
    wo = gather(wout, 1)
    fup = pick(gather(wup, 1).reshape(L, D, z.dp, TP, z.fc), 3, pos).reshape(L, D, z.fs)
    fdn = pick(gather(wdown, 1).reshape(L, z.dp, TP, z.fc, D), 2, pos).reshape(L, z.fs, D)
    latcot = jnp.stack([latents, cotangent], axis=1).astype(z.lt)
    lat, gm, gla, gqkv, gout, gup, gdn, gn = call(z, media.astype(z.mt), latcot, counts, nrm, wqkv, wo, fup, fdn)

    def spread(g, shape, axis, index):
        full = jnp.zeros(shape, F32)
        return lax.dynamic_update_index_in_dim(full, g.astype(F32), index, axis)

    scat = lambda g: lax.psum_scatter(g, BOTH, scatter_dimension=1, tiled=True)
    gq = scat(spread(gqkv[:, :, : z.half], (L, D, 2, z.half), 2, c).reshape(L, D, z.inner))
    gkv = spread(gqkv[:, :, z.half :].reshape(L, D, 2, z.half), (L, D, 2, 2, z.half), 3, c)
    gkv = scat(gkv.reshape(L, D, 2 * z.inner))
    go = scat(spread(gout, (L, z.inner, 2, D // 2), 2, c).reshape(L, z.inner, D))
    gu = spread(gup.reshape(L, D, z.dp, z.fc), (L, D, z.dp, TP, z.fc), 3, pos)
    gu = scat(gu.reshape(L, D, z.ff))
    gd = spread(gdn.reshape(L, z.dp, z.fc, D), (L, z.dp, TP, z.fc, D), 2, pos)
    gd = scat(gd.reshape(L, z.ff, D))
    gnr = lax.psum_scatter(gn, BOTH, scatter_dimension=1, tiled=True)[: 6 * L].reshape(L, 6, -1)
    return lat.astype(BF), gm.astype(F32), gla, gq, gkv, go, gu, gd, gnr


def solution(mesh):
    rows = P("img", "seq", None)
    weight = P(None, BOTH, None)
    return jax.shard_map(
        functools.partial(body, mesh),
        mesh=mesh,
        in_specs=(rows, rows, P("img"), weight, weight, weight, weight, weight, P(None, None, BOTH), rows),
        out_specs=(rows, rows, rows, weight, weight, weight, weight, weight, P(None, None, BOTH)),
        check_vma=False,
    )
```

```python
import functools
import types

import jax
import jax.numpy as jnp
from jax import lax
from jax.experimental import pallas as pl
from jax.experimental.pallas import tpu as pltpu
from jax.sharding import PartitionSpec as P

HEAD = 64
EPS = 1e-05
MESH = pl.DeviceIdType.MESH
BF = jnp.bfloat16
F32 = jnp.float32
TP = 8
BOTH = ("img", "seq")


class Sizes:
    def __init__(self, mesh, media, latents, wq, wkv, wout, wup, wdown):
        self.ni, self.ns = mesh.shape["img"], mesh.shape["seq"]
        self.ny = self.ns // 2
        self.chips = self.ni * self.ny
        self.layers = wq.shape[0]
        self.d = media.shape[2]
        self.nimg, self.pr = media.shape[0], media.shape[1]
        self.lr = latents.shape[1]
        self.inner = wq.shape[2]
        self.half = self.inner // 2
        self.ff = wup.shape[2]
        self.fs = self.ff // TP
        self.dp = self.chips // TP
        self.fc = self.ff // self.chips
        self.pm = self.pr * self.ns
        self.latn = self.lr * self.ns
        self.r = self.latn // 2
        self.keys = self.pm + self.latn
        self.heads = self.half // HEAD
        self.rows = TP * self.r
        self.mt = BF if self.pr % 16 == 0 else F32
        self.lt = BF if self.lr % 16 == 0 else F32
        self.rq, self.ro, self.rd = wq.shape[1], wout.shape[1], wdown.shape[1]
        self.lanes = self.d // self.ni
        whole_tiles = all(v % 16 == 0 for v in (self.rq, self.ro, self.rd))
        whole_tiles = whole_tiles and self.fc % 128 == 0 and self.lanes % 128 == 0
        self.fused = whole_tiles and self.ny == 2 and self.ni % 4 == 0
        self.blk = (self.ni // 2, 2, self.ny) if self.fused else (2, 1, 1)
        self.nblk = self.blk[0] * self.blk[1] * self.blk[2]
        self.qrows = self.d // self.nblk
        self.orows = self.inner // self.nblk
        self.wide = 3 * self.half + self.d // 4
        assert self.nimg == self.ny and TP % self.ny == 0


def dot(a, b, ca=1, cb=0):
    return lax.dot_general(a, b, (((ca,), (cb,)), ((), ())), preferred_element_type=F32)


def centre(v):
    c = v - jnp.mean(v, axis=-1, keepdims=True)
    rstd = lax.rsqrt(jnp.mean(c * c, axis=-1, keepdims=True) + EPS)
    return c * rstd, rstd


def pull(xhat, rstd, cot, gain):
    g = cot * gain
    m1 = jnp.mean(g, axis=-1, keepdims=True)
    m2 = jnp.mean(g * xhat, axis=-1, keepdims=True)
    return rstd * (g - m1 - xhat * m2)


def col_sum(v):
    return jnp.sum(v, axis=0, keepdims=True)


def inputs_of(z):
    any_ = pl.ANY
    names = [("media_in", any_), ("latcot_in", any_), ("counts", pltpu.SMEM), ("nrm_in", any_)]
    if z.fused:
        names += [("wq_in", any_), ("wkv_in", any_), ("wo_in", any_), ("wup_in", any_), ("wdn_in", any_)]
    else:
        names += [("wqkv_in", any_), ("wo_in", any_), ("wup_in", any_), ("wdn_in", any_)]
    return names


def outputs_of(z):
    L, D = z.layers, z.d
    outs = dict(
        lat_out=(pl.ANY, (z.ny, z.lr, D), z.lt),
        gmedia_out=(pl.ANY, (z.ny, z.pr, D), z.mt),
        glat_out=(pl.ANY, (z.ny, z.lr, D), F32),
    )
    if z.fused:
        outs.update(
            gq_out=(pltpu.VMEM, (L, z.rq, z.inner), F32),
            gkv_out=(pltpu.VMEM, (L, z.rq, 2 * z.inner), F32),
            go_out=(pltpu.VMEM, (L, z.ro, D), F32),
            gup_out=(pltpu.VMEM, (L, z.rq, z.ff), F32),
            gdn_out=(pltpu.VMEM, (L, z.rd, D), F32),
            gn_out=(pltpu.VMEM, (16, z.lanes), F32),
        )
    else:
        outs.update(
            gat_out=(pl.ANY, (L, *z.blk, z.qrows, z.wide), BF),
            gup_out=(pl.ANY, (L, z.chips if z.fused else 1, 2, D // 2 if not z.fused else z.rq, z.fs), BF),
            gdn_out=(pl.ANY, (L, 1, 2, z.fs // 2, D), BF),
            gn_out=(pltpu.VMEM, (16, D), F32),
        )
    return outs


def scratch_of(z):
    L, D, R, T = z.layers, z.d, z.r, TP
    kq = z.heads * z.latn
    cu = z.chips if z.fused else 1
    gd = z.dp if z.fused else 1
    v = dict(
        media=((z.ns, z.pr, D), z.mt),
        lc=((z.ny, 2, z.lr, D), z.lt),
        mn=((L, z.keys, D), BF),
        kv=((L, z.keys, 2 * z.half), BF),
        wqkv=((L, *z.blk, z.qrows, 3 * z.half), BF),
        wo=((L, *z.blk, 2, z.orows // 2, D), BF),
        wup=((L, cu, 2, D // (2 * cu), z.fs), BF),
        wdn=((L, gd, 2, z.fs // (2 * gd), D), BF),
        nrm=((16, D), F32),
        q4=((L, kq, z.half), BF),
        pexp=((L, kq, z.keys), F32),
        rtot=((L, kq, 1), F32),
        att4=((L, z.latn, z.half), F32),
        atta=((L, 2, z.latn, z.half), BF),
        aft=((L, R, D), F32),
        ffa=((L, T, R, D), BF),
        hp=((L, z.rows, z.fs), F32),
        act=((L, z.rows, z.fs), BF),
        xs=((L, R, D), F32),
        gza=((L, T, R, D), BF),
        psend=((2 * L, T, R, D), BF),
        precv=((2 * L, T, R, D), BF),
        gpre=((L, z.rows, z.fs), BF),
        gya=((L, 2, R, D), BF),
        gl=((L, 2, R, D), F32),
        grecv=((L, R, D), F32),
        gkvm=((L, z.keys, 2 * z.half), BF),
        macc=((z.pm, D), F32),
        msend=((z.pm // 2, D), z.mt),
        mrecv=((z.pm // 2, D), z.mt),
        gn=((16, D), F32),
        xout=((z.ny, z.lr, D), z.lt),
        gxo=((z.ny, z.lr, D), F32),
        cm=((z.pm, D), F32),
        fold=((kq, z.half), F32),
        gat=((L, *z.blk, z.qrows, z.wide), BF),
        gup=((L, cu, 2, D // (2 * cu), z.fs), BF),
        gdn=((L, gd, 2, z.fs // (2 * gd), D), BF),
    )
    if z.fused:
        za = z.blk[0]
        v.update(
            nrecv=((z.ni, z.ns, 16, z.lanes), BF),
            ra=((L, za, 2, z.qrows, z.wide), BF),
            sa=((L, za, 2, z.qrows, z.wide), BF),
            rb=((L, za, z.qrows, z.wide), BF),
            sb=((L, za, z.qrows, z.wide), BF),
            rc=((L, za, z.qrows, z.wide), BF),
            sf=((L, z.qrows, z.wide), F32),
            rf=((L, z.qrows, z.wide), F32),
            updr=((L, z.chips, z.rq, z.fs), BF),
            ups=((L, z.chips, z.rq, z.fs), BF),
            upr=((L, z.chips, z.rq, z.fs), BF),
            dndr=((L, z.dp, z.rd, D), BF),
            dns=((L, z.dp, z.rd, D), BF),
            dnr=((L, z.dp, z.rd, D), BF),
            gns=((16, D), F32),
            gnd=((16, D), F32),
            gnr=((z.chips, 16, z.lanes), F32),
        )
    out = {n: pltpu.VMEM(s, d) for n, (s, d) in v.items()}
    out.update(ss=pltpu.SemaphoreType.DMA((NSEM,)), rs=pltpu.SemaphoreType.DMA((NSEM,)), ls=pltpu.SemaphoreType.DMA((16,)))
    return out


NSEM = 80


def kernel(z, names, *refs):
    L = z.layers
    q = types.SimpleNamespace(**dict(zip(names, refs)))
    ss, rs, ls = q.ss, q.rs, q.ls
    i = lax.axis_index("img")
    s = lax.axis_index("seq")
    y, c = s // 2, s % 2
    k = i * z.ny + y
    pos, grp = k % TP, k // TP
    sib = (i, y * 2 + (1 - c))
    a, b = i // 2, i % 2

    def chip(kk, cc):
        return (kk // z.ny, (kk % z.ny) * 2 + cc)

    def peer(t):
        return chip(grp * TP + (pos + t) % TP, c)

    waits = []
    used = [0]

    def sem():
        used[0] += 1
        return used[0] - 1

    def send(src, dst, dev, n):
        pltpu.make_async_remote_copy(src, dst, ss.at[n], rs.at[n], device_id=dev, device_id_type=MESH).start()

    def keep(src, dst, n):
        pltpu.make_async_copy(src, dst, rs.at[n]).start()

    def arrive(ref, n):
        pltpu.make_async_copy(ref, ref, rs.at[n]).wait()

    def gone(ref, n):
        pltpu.make_async_copy(ref, ref, ss.at[n]).wait()

    def sent(ref, n):
        waits.append((ref, n))

    bar = pltpu.get_barrier_semaphore()
    total = z.ni * z.ns
    me = i * z.ns + s

    def greet(t, _):
        o = (me + t) % total
        pl.semaphore_signal(bar, inc=1, device_id=(o // z.ns, o % z.ns), device_id_type=MESH)
        return 0

    lax.fori_loop(1, total, greet, 0)
    pl.semaphore_wait(bar, total - 1)

    def lanes(start, size):
        return pl.ds(pl.multiple_of(start, 128), size)

    def at16(start, size):
        return pl.ds(pl.multiple_of(start, 16), size)

    H = z.half
    if z.fused:
        za = z.blk[0]
        n_w0, n_q1, n_q2, n_q3 = ([sem() for _ in range(L)] for _ in range(4))
        n_o0, n_o1, n_o2, n_o3, n_od = ([sem() for _ in range(L)] for _ in range(5))
        n_ua, n_ub, n_da, n_db = ([sem() for _ in range(L)] for _ in range(4))
        n_nrm = sem()
        xdev = (i + 1 - 2 * b, s)
        ydev = (i, (1 - y) * 2 + c)
        first = (xdev[0] * (1 - c) + i * c, s * (1 - c) + ydev[1] * c)
        second = (i * (1 - c) + xdev[0] * c, ydev[1] * (1 - c) + s * c)

        def weights_pair(l):
            rows = at16(c * z.rq, z.rq)
            block = q.wqkv.at[l, a, b, y, rows]
            for cc, dev in ((c, None), (1 - c, sib)):
                for src, off in ((q.wq_in.at[l, :, lanes(cc * H, H)], 0), (q.wkv_in.at[l, :, lanes(cc * H, H)], H),
                                 (q.wkv_in.at[l, :, lanes(z.inner + cc * H, H)], 2 * H)):
                    dst = block.at[:, pl.ds(off, H)]
                    if dev is None:
                        keep(src, dst, n_w0[l])
                    else:
                        send(src, dst, dev, n_w0[l])
            sent(q.wqkv.at[l, 0, 0, 0, pl.ds(0, z.rq)], n_w0[l])
            keep(q.wo_in.at[l], q.wo.at[l, a, b, y, c], n_o0[l])

        def weights_z(l):
            arrive(q.wqkv.at[l, a, b, y], n_w0[l])
            for t in range(1, za):
                dev = (((a + t) % za) * 2 + b, s)
                send(q.wqkv.at[l, a, b, y], q.wqkv.at[l, a, b, y], dev, n_q1[l])
            arrive(q.wo.at[l, a, b, y, c], n_o0[l])
            for t in range(1, za):
                dev = (((a + t) % za) * 2 + b, s)
                send(q.wo.at[l, a, b, y, c], q.wo.at[l, a, b, y, c], dev, n_o1[l])

        def weights_first(l):
            part = q.wqkv.at[l, pl.ds(0, za - 1), 0, 0]
            arrive(part, n_q1[l])
            sent(part, n_q1[l])
            send(q.wqkv.at[l, :, b, y], q.wqkv.at[l, :, b, y], first, n_q2[l])
            part = q.wo.at[l, pl.ds(0, za - 1), 0, 0, 0]
            arrive(part, n_o1[l])
            sent(part, n_o1[l])
            send(q.wo.at[l, :, b, y, c], q.wo.at[l, :, b, y, c], first, n_o2[l])

        def weights_second(l):
            for buf, n2, n3, tail in ((q.wqkv, n_q2[l], n_q3[l], ()), (q.wo, n_o2[l], n_o3[l], (c,))):
                part = buf.at[(l, slice(None), 0, 0) + ((0,) if tail else ())]
                arrive(part, n2)
                sent(part, n2)
                mid = (slice(None),) * 2 if tail else ()

                @pl.when(c == 0)
                def _():
                    ref = buf.at[(l, slice(None), slice(None), y) + ((0,) if tail else ())]
                    send(ref, ref, second, n3)

                @pl.when(c == 1)
                def _():
                    ref = buf.at[(l, slice(None), b) + ((slice(None), 1) if tail else ())]
                    send(ref, ref, second, n3)

        def weights_qkv_end(l):
            part = q.wqkv.at[l, :, 0]
            arrive(part, n_q3[l])
            sent(part, n_q3[l])

        def weights_out_share(l):
            part = q.wo.at[l, :, 0, :, 0]
            arrive(part, n_o3[l])
            sent(part, n_o3[l])
            ref = q.wo.at[l, :, :, :, c]
            send(ref, ref, sib, n_od[l])

        def weights_out_end(l):
            ref = q.wo.at[l, :, :, :, 0]
            arrive(ref, n_od[l])
            sent(ref, n_od[l])

        def weights_ff(l):
            def one(t, _):
                kk = (k + t) % z.chips
                dev = chip(kk, c)
                for g in range(z.dp):
                    src = q.wup_in.at[l, :, lanes((g * TP + kk % TP) * z.fc, z.fc)]
                    send(src, q.wup.at[l, k, c, :, pl.ds(g * z.fc, z.fc)], dev, n_ua[l])
                return 0

            for g in range(1, z.dp):
                dev = chip(((grp + g) % z.dp) * TP + pos, c)
                send(q.wdn_in.at[l], q.wdn.at[l, grp, c], dev, n_da[l])
            keep(q.wdn_in.at[l], q.wdn.at[l, grp, c], n_da[l])
            lax.fori_loop(1, z.chips, one, 0)
            for g in range(z.dp):
                src = q.wup_in.at[l, :, lanes((g * TP + pos) * z.fc, z.fc)]
                keep(src, q.wup.at[l, k, c, :, pl.ds(g * z.fc, z.fc)], n_ua[l])
            sent(q.wup.at[l, pl.ds(0, z.chips - 1), 0], n_ua[l])
            sent(q.wdn.at[l, pl.ds(0, z.dp - 1), 0], n_da[l])

        def weights_ff_share(l):
            arrive(q.wup.at[l, :, 0], n_ua[l])
            send(q.wup.at[l, :, c], q.wup.at[l, :, c], sib, n_ub[l])
            arrive(q.wdn.at[l, :, 0], n_da[l])
            send(q.wdn.at[l, :, c], q.wdn.at[l, :, c], sib, n_db[l])

        def weights_ff_end(l):
            arrive(q.wup.at[l, :, 0], n_ub[l])
            sent(q.wup.at[l, :, 0], n_ub[l])
            arrive(q.wdn.at[l, :, 0], n_db[l])
            sent(q.wdn.at[l, :, 0], n_db[l])

        def norms_start():
            def one(t, _):
                o = (me + t) % total
                send(q.nrm_in, q.nrecv.at[i, s], (o // z.ns, o % z.ns), n_nrm)
                return 0

            lax.fori_loop(1, total, one, 0)
            keep(q.nrm_in, q.nrecv.at[i, s], n_nrm)

        def norms_end():
            arrive(q.nrecv, n_nrm)
            for ii in range(z.ni):
                v = q.nrecv[ii, 0].astype(F32)
                for j in range(1, z.ns):
                    v = v + q.nrecv[ii, j].astype(F32)
                q.nrm[:, ii * z.lanes:(ii + 1) * z.lanes] = v
    else:
        loads = [(q.nrm_in, q.nrm)]
        for l in range(L):
            loads += [(getattr(q, n + "_in").at[l], getattr(q, n).at[l]) for n in ("wqkv", "wo", "wup", "wdn")]

        def norms_start():
            for n, (src, dst) in enumerate(loads):
                pltpu.make_async_copy(src, dst, ls.at[n]).start()

        def load_end(n):
            pltpu.make_async_copy(*loads[n], ls.at[n]).wait()

        def norms_end():
            load_end(0)

        def nothing(l):
            pass

        weights_pair = weights_z = weights_first = weights_second = nothing
        weights_out_share = weights_ff = weights_ff_share = nothing

        def weights_qkv_end(l):
            load_end(1 + 4 * l)

        def weights_out_end(l):
            load_end(2 + 4 * l)

        def weights_ff_end(l):
            load_end(3 + 4 * l)
            load_end(4 + 4 * l)

    def w_qkv(l):
        return q.wqkv[l].reshape(z.d, 3 * H)

    def w_kv(l):
        return q.wqkv[l, :, :, :, :, H:].reshape(z.d, 2 * H)

    def w_up(l):
        return q.wup[l].reshape(z.d, z.fs)

    def w_dn(l):
        return q.wdn[l].reshape(z.fs, z.d)

    n_lc, n_ma, n_mb = sem(), sem(), sem()
    n_ff, n_gz, n_ln, n_at, n_gy, n_gl = ([sem() for _ in range(L)] for _ in range(6))
    n_rs = [sem() for _ in range(2 * L)]
    n_md, n_lo, n_go, n_mo = sem(), sem(), sem(), sem()
    own_slot = s % z.ny

    def rows_start():
        for t in range(1, z.ny):
            yy = (y + t) % z.ny
            send(q.media_in.at[yy], q.media.at[s], (i, yy * 2 + c), n_ma)
        keep(q.media_in.at[y], q.media.at[s], n_ma)
        send(q.media_in.at[y], q.media.at[s], sib, n_mb)
        for yy in range(z.ny):
            to = yy * 2 + s // z.ny

            @pl.when(to != s)
            def _():
                send(q.latcot_in.at[yy], q.lc.at[own_slot], (i, to), n_lc)

            @pl.when(to == s)
            def _():
                keep(q.latcot_in.at[yy], q.lc.at[own_slot], n_lc)

    def media_share():
        arrive(q.media.at[pl.ds(0, z.ny)], n_ma)
        for t in range(1, z.ny):
            yy = (y + t) % z.ny
            send(q.media.at[yy * 2 + c], q.media.at[yy * 2 + c], sib, n_mb)

    def rows_sent():
        for yy in range(z.ny):
            @pl.when(yy * 2 + s // z.ny != s)
            def _():
                gone(q.lc.at[0], n_lc)
        if z.ny > 1:
            gone(q.media.at[pl.ds(0, z.ny - 1)], n_ma)
        gone(q.media.at[pl.ds(0, z.ny)], n_mb)

    def gather_start(buf, value, n):
        buf[pos] = value
        for t in range(1, TP):
            send(buf.at[pos], buf.at[pos], peer(t), n)

    def gather_end(buf, n):
        arrive(buf.at[pl.ds(0, TP - 1)], n)
        sent(buf.at[pl.ds(0, TP - 1)], n)

    def swap(ref, value, n):
        ref[...] = value
        send(ref, ref, sib, n)
        arrive(ref, n)
        sent(ref, n)

    def scatter_sum(part, j):
        q.psend[j] = part.astype(BF).reshape(TP, z.r, z.d)
        for t in range(1, TP):
            o = (pos + t) % TP
            send(q.psend.at[j, o], q.precv.at[j, pos], peer(t), n_rs[j])
        q.precv[j, pos] = q.psend[j, pos]

    def scatter_end(j):
        arrive(q.precv.at[j, pl.ds(0, TP - 1)], n_rs[j])
        sent(q.precv.at[j, pl.ds(0, TP - 1)], n_rs[j])
        out = q.precv[j, 0].astype(F32)
        for t in range(1, TP):
            out = out + q.precv[j, t].astype(F32)
        return out

    def vec(l, m):
        return q.nrm[6 * l + m][None, :]

    lane_head = lax.broadcasted_iota(jnp.int32, (1, H), 1) // HEAD

    def stack_heads(v):
        return jnp.concatenate([jnp.where(lane_head == h, v, jnp.zeros_like(v)) for h in range(z.heads)], axis=0)

    def fold_heads(v):
        out = None
        q.fold[...] = v
        for h in range(z.heads):
            part = jnp.where(lane_head == h, q.fold[h * z.latn:(h + 1) * z.latn], 0.0)
            out = part if out is None else out + part
        return out

    key_pos = lax.broadcasted_iota(jnp.int32, (1, z.keys), 1)
    live = (key_pos < q.counts[y]) | (key_pos >= z.pm)

    def norm_piece(j, _):
        xhat, _ = centre(q.media[j].astype(F32))
        rows = pl.ds(pl.multiple_of(j * z.pr, 8), z.pr)
        for l in range(L):
            q.mn[l, rows] = (xhat * vec(l, 0) + vec(l, 1)).astype(BF)
        return 0

    def media_kv(l):
        q.kv[l, :z.pm] = dot(q.mn[l, :z.pm], w_kv(l)).astype(BF)

    def attention(l):
        xhat, _ = centre(q.xs[l])
        swap(q.mn.at[l, at16(z.pm + c * z.r, z.r)], (xhat * vec(l, 2) + vec(l, 3)).astype(BF), n_ln[l])
        qkv = dot(q.mn[l, z.pm:], w_qkv(l)).astype(BF)
        q.kv[l, z.pm:] = qkv[:, H:]
        queries = stack_heads(qkv[:, :H])
        q.q4[l] = queries
        scores = dot(queries, q.kv[l, :, :H], 1, 1) * 0.125
        scores = jnp.where(live, scores, -1000000000.0)
        e = jnp.exp(scores - jnp.max(scores, axis=-1, keepdims=True))
        rt = jnp.sum(e, axis=-1, keepdims=True)
        q.pexp[l] = e
        q.rtot[l] = rt
        own = fold_heads(dot(e.astype(BF), q.kv[l, :, H:]) / rt)
        q.att4[l] = own
        swap(q.atta.at[l, c], own.astype(BF), n_at[l])

    def attention_out(l):
        mine = at16(c * z.r, z.r)
        att = jnp.concatenate([q.atta[l, 0, mine], q.atta[l, 1, mine]], axis=1)
        after = q.xs[l] + dot(att, q.wo[l].reshape(z.inner, z.d))
        q.aft[l] = after
        xhat, _ = centre(after)
        gather_start(q.ffa.at[l], (xhat * vec(l, 4) + vec(l, 5)).astype(BF), n_ff[l])

    def hidden(l):
        h = dot(q.ffa[l].reshape(z.rows, z.d), w_up(l))
        q.hp[l] = h
        q.act[l] = (h * (0.5 * (1.0 + lax.erf(h * 0.7071067811865476)))).astype(BF)

    def down(l):
        scatter_sum(dot(q.act[l], w_dn(l)), l)

    def ff_back(l):
        gather_end(q.gza.at[l], n_gz[l])
        g = dot(q.gza[l].reshape(z.rows, z.d), w_dn(l), 1, 1)
        h = q.hp[l]
        slope = 0.5 * (1.0 + lax.erf(h * 0.7071067811865476)) + h * 0.3989422804014327 * jnp.exp(-0.5 * h * h)
        q.gpre[l] = (g * slope).astype(BF)
        scatter_sum(dot(q.gpre[l], w_up(l), 1, 1), L + l)

    def ff_grads(l):
        q.gdn[l] = dot(q.act[l], q.gza[l].reshape(z.rows, z.d), 0, 0).astype(BF).reshape(q.gdn.shape[1:])
        q.gup[l] = dot(q.ffa[l].reshape(z.rows, z.d), q.gpre[l], 0, 0).astype(BF).reshape(q.gup.shape[1:])

    def attn_back(l, gx):
        gff = scatter_end(L + l)
        xhat, rstd = centre(q.aft[l])
        q.gn[6 * l + 4] = jnp.sum(gff * xhat, axis=0)
        q.gn[6 * l + 5] = jnp.sum(gff, axis=0)
        gafter = gx + pull(xhat, rstd, gff, vec(l, 4))
        swap(q.gya.at[l, c], gafter.astype(BF), n_gy[l])
        gy = q.gya[l].reshape(z.latn, z.d)
        hb = z.blk[0] // 2
        wo_own = q.wo[l, pl.ds(c * hb, hb)].reshape(H, z.d)
        gatt = dot(gy, wo_own, 1, 1).astype(BF)
        g4 = stack_heads(gatt.astype(F32))
        delta = jnp.sum(g4 * stack_heads(q.att4[l]), axis=-1, keepdims=True)
        rt = q.rtot[l]
        e = q.pexp[l]
        gp = dot(g4.astype(BF), q.kv[l, :, H:], 1, 1)
        gs = (e / rt * (gp - delta)).astype(BF)
        gq = (fold_heads(dot(gs, q.kv[l, :, :H])) * 0.125).astype(BF)
        gk = (dot(gs, q.q4[l], 0, 0) * 0.125).astype(BF)
        gv = dot(e.astype(BF), (g4 / rt).astype(BF), 0, 0).astype(BF)
        glat = jnp.concatenate([gq, gk[z.pm:], gv[z.pm:]], axis=1)
        q.gl[l] = dot(glat, w_qkv(l), 1, 1).reshape(2, z.r, z.d)
        send(q.gl.at[l, 1 - c], q.grecv.at[l], sib, n_gl[l])
        q.gkvm[l, :, :H] = gk
        q.gkvm[l, :, H:] = gv
        arrive(q.grecv.at[l], n_gl[l])
        sent(q.grecv.at[l], n_gl[l])
        gln = q.gl[l, c] + q.grecv[l]
        xhat, rstd = centre(q.xs[l])
        q.gn[6 * l + 2] = jnp.sum(gln * xhat, axis=0)
        q.gn[6 * l + 3] = jnp.sum(gln, axis=0)
        return gafter + pull(xhat, rstd, gln, vec(l, 2)), gq

    def attn_grads(l, gq):
        to = q.gat.at[l]
        shape = (*z.blk, z.qrows)
        to[:, :, :, :, :H] = dot(q.mn[l, z.pm:], gq, 0, 0).astype(BF).reshape(*shape, H)
        to[:, :, :, :, H:3 * H] = dot(q.mn[l], q.gkvm[l], 0, 0).astype(BF).reshape(*shape, 2 * H)
        att = jnp.concatenate([q.atta[l, 0], q.atta[l, 1]], axis=1)
        cols = lanes(c * (z.d // 2), z.d // 2)
        gyc = jnp.concatenate([q.gya[l, 0, :, cols], q.gya[l, 1, :, cols]], axis=0)
        g = dot(att, gyc, 0, 0).astype(BF).reshape(*z.blk, z.orows, z.d // 2)
        to[:, :, :, :z.orows, 3 * H:] = g[..., :z.d // 4]
        to[:, :, :, z.orows:2 * z.orows, 3 * H:] = g[..., z.d // 4:]

    def media_back(l):
        q.cm[...] = dot(q.gkvm[l, :z.pm], w_kv(l), 1, 1)

        def piece(j, sums):
            rows = pl.ds(pl.multiple_of(j * z.pr, 8), z.pr)
            xhat, rstd = centre(q.media[j].astype(F32))
            cotm = q.cm[rows]
            add = cotm * vec(l, 0)
            q.macc[rows] = add if l == L - 1 else q.macc[rows] + add
            return sums[0] + col_sum(cotm * xhat), sums[1] + col_sum(cotm)

        zero = jnp.zeros((1, z.d), F32)
        u, v = lax.fori_loop(0, z.ns, piece, (zero, zero))
        q.gn[6 * l + 0] = u[0]
        q.gn[6 * l + 1] = v[0]

    if z.fused:
        n_ra, n_rb, n_rc, n_rf, n_ud, n_us, n_dd, n_ds = ([sem() for _ in range(L)] for _ in range(8))
        n_nd, n_ns = sem(), sem()

        def add_to(dst, x, w):
            dst[...] = (x[...].astype(F32) + w[...].astype(F32)).astype(BF)

        def grads_first(l):
            @pl.when(c == 0)
            def _():
                send(q.gat.at[l, :, :, 1 - y], q.ra.at[l], second, n_ra[l])

            @pl.when(c == 1)
            def _():
                send(q.gat.at[l, :, 1 - b], q.ra.at[l], second, n_ra[l])

        def grads_second(l):
            arrive(q.ra.at[l], n_ra[l])
            sent(q.ra.at[l], n_ra[l])

            @pl.when(c == 0)
            def _():
                add_to(q.sa.at[l], q.gat.at[l, :, :, y], q.ra.at[l])
                send(q.sa.at[l, :, 1 - b], q.rb.at[l], first, n_rb[l])

            @pl.when(c == 1)
            def _():
                add_to(q.sa.at[l], q.gat.at[l, :, b], q.ra.at[l])
                send(q.sa.at[l, :, 1 - y], q.rb.at[l], first, n_rb[l])

        def grads_third(l):
            arrive(q.rb.at[l], n_rb[l])
            sent(q.rb.at[l], n_rb[l])
            add_to(q.sb.at[l], q.sa.at[l, :, b * (1 - c) + y * c], q.rb.at[l])
            for t in range(1, za):
                o = (a + t) % za
                send(q.sb.at[l, o], q.rc.at[l, a], (o * 2 + b, s), n_rc[l])
            q.rc[l, a] = q.sb[l, a]

        def grads_last(l):
            part = q.rc.at[l, pl.ds(0, za - 1)]
            arrive(part, n_rc[l])
            sent(part, n_rc[l])
            v = q.rc[l, 0].astype(F32)
            for t in range(1, za):
                v = v + q.rc[l, t].astype(F32)
            q.sf[l] = v
            send(q.sf.at[l], q.rf.at[l], sib, n_rf[l])

        def grads_out(l):
            arrive(q.rf.at[l], n_rf[l])
            sent(q.rf.at[l], n_rf[l])
            for buf, cc in ((q.sf, c), (q.rf, 1 - c)):
                v = buf[l, at16(c * z.rq, z.rq), :3 * H]
                q.gq_out[l, :, lanes(cc * H, H)] = v[:, :H]
                q.gkv_out[l, :, lanes(cc * H, H)] = v[:, H:2 * H]
                q.gkv_out[l, :, lanes(z.inner + cc * H, H)] = v[:, 2 * H:]
                for part in range(2):
                    rows = at16(part * z.orows + c * z.ro, z.ro)
                    col = cc * (z.d // 2) + part * (z.d // 4)
                    q.go_out[l, :, lanes(col, z.d // 4)] = buf[l, rows, 3 * H:]

        def ff_pair(l):
            send(q.gup.at[l, :, 1 - c], q.updr.at[l], sib, n_ud[l])
            send(q.gdn.at[l, :, 1 - c], q.dndr.at[l], sib, n_dd[l])

        def ff_spread(l):
            arrive(q.dndr.at[l], n_dd[l])
            sent(q.dndr.at[l], n_dd[l])
            add_to(q.dns.at[l], q.gdn.at[l, :, c], q.dndr.at[l])
            for g in range(1, z.dp):
                o = (grp + g) % z.dp
                send(q.dns.at[l, o], q.dnr.at[l, grp], chip(o * TP + pos, c), n_ds[l])
            arrive(q.updr.at[l], n_ud[l])
            sent(q.updr.at[l], n_ud[l])
            add_to(q.ups.at[l], q.gup.at[l, :, c], q.updr.at[l])

            def one(t, _):
                kk = (k + t) % z.chips
                send(q.ups.at[l, kk], q.upr.at[l, k], chip(kk, c), n_us[l])
                return 0

            lax.fori_loop(1, z.chips, one, 0)
            q.dnr[l, grp] = q.dns[l, grp]
            q.upr[l, k] = q.ups[l, k]

        def ff_out(l):
            part = q.dnr.at[l, pl.ds(0, z.dp - 1)]
            arrive(part, n_ds[l])
            sent(part, n_ds[l])
            v = q.dnr[l, 0].astype(F32)
            for g in range(1, z.dp):
                v = v + q.dnr[l, g].astype(F32)
            q.gdn_out[l] = v
            part = q.upr.at[l, pl.ds(0, z.chips - 1)]
            arrive(part, n_us[l])
            sent(part, n_us[l])
            for p in range(TP):
                v = q.upr[l, p].astype(F32)
                for g in range(1, z.dp):
                    v = v + q.upr[l, g * TP + p].astype(F32)
                for g in range(z.dp):
                    col = (g * TP + p) * z.fc
                    q.gup_out[l, :, col:col + z.fc] = v[:, g * z.fc:(g + 1) * z.fc]

        def norms_pair():
            send(q.gn, q.gnd, sib, n_nd)

        def norms_spread():
            arrive(q.gnd, n_nd)
            sent(q.gnd, n_nd)
            q.gns[...] = q.gn[...] + q.gnd[...]

            def one(t, _):
                kk = (k + t) % z.chips
                dev = chip(kk, c)
                send(q.gns.at[:, lanes(dev[0] * z.lanes, z.lanes)], q.gnr.at[k], dev, n_ns)
                return 0

            lax.fori_loop(1, z.chips, one, 0)
            q.gnr[k] = q.gns[:, lanes(i * z.lanes, z.lanes)]

        def norms_out():
            part = q.gnr.at[pl.ds(0, z.chips - 1)]
            arrive(part, n_ns)
            sent(part, n_ns)
            v = q.gnr[0]
            for t in range(1, z.chips):
                v = v + q.gnr[t]
            q.gn_out[...] = v
    else:
        def grads_first(l):
            pltpu.make_async_copy(q.gat.at[l], q.gat_out.at[l], ls.at[9 + l]).start()

        def grads_out(l):
            pltpu.make_async_copy(q.gat.at[l], q.gat_out.at[l], ls.at[9 + l]).wait()

        def ff_pair(l):
            pltpu.make_async_copy(q.gup.at[l], q.gup_out.at[l], ls.at[11 + l]).start()
            pltpu.make_async_copy(q.gdn.at[l], q.gdn_out.at[l], ls.at[13 + l]).start()

        def ff_out(l):
            pltpu.make_async_copy(q.gup.at[l], q.gup_out.at[l], ls.at[11 + l]).wait()
            pltpu.make_async_copy(q.gdn.at[l], q.gdn_out.at[l], ls.at[13 + l]).wait()

        grads_second = grads_third = grads_last = ff_spread = nothing

        def norms_pair():
            pass

        def norms_spread():
            pass

        def norms_out():
            q.gn_out[...] = q.gn[...]

    for l in range(L):
        weights_pair(l)
    rows_start()
    norms_start()
    weights_z(0)
    arrive(q.lc, n_lc)
    cot = q.lc[:, 1].astype(F32).reshape(z.r, z.d)
    q.xs[0] = q.lc[:, 0].astype(F32).reshape(z.r, z.d)
    norms_end()
    media_share()
    weights_first(0)
    weights_ff(0)
    arrive(q.media.at[pl.ds(0, z.ny)], n_mb)
    lax.fori_loop(0, z.ns, norm_piece, 0)
    weights_second(0)
    gather_start(q.gza.at[L - 1], cot.astype(BF), n_gz[L - 1])
    weights_qkv_end(0)
    media_kv(0)
    for l in range(L):
        if l + 1 < L:
            weights_z(l + 1)
        attention(l)
        weights_out_share(l)
        weights_out_end(l)
        attention_out(l)
        weights_ff_share(l)
        if l + 1 < L:
            weights_first(l + 1)
            weights_ff(l + 1)
        weights_ff_end(l)
        gather_end(q.ffa.at[l], n_ff[l])
        hidden(l)
        if l + 1 < L:
            down(l)
            weights_second(l + 1)
            q.xs[l + 1] = q.aft[l] + scatter_end(l)
            weights_qkv_end(l + 1)
            media_kv(l + 1)
    gx = cot
    for l in reversed(range(L)):
        if l < L - 1:
            gather_start(q.gza.at[l], gx.astype(BF), n_gz[l])
            attn_grads(l + 1, gq)
            grads_first(l + 1)
            media_back(l + 1)
            q.xout[...] = (q.aft[L - 1] + scatter_end(L - 1)).astype(z.lt).reshape(z.ny, z.lr, z.d)
        ff_back(l)
        if l == L - 1:
            down(l)
        ff_grads(l)
        ff_pair(l)
        if l < L - 1:
            ff_spread(l + 1)
            grads_second(l + 1)
        gx, gq = attn_back(l, gx)
    attn_grads(0, gq)
    grads_first(0)
    for l in range(1, L):
        grads_third(l)
    ff_spread(0)
    q.gxo[...] = gx.reshape(z.ny, z.lr, z.d)

    def give_back(srcs, out, n):
        for j in range(z.ny):
            to = c * z.ny + j

            @pl.when(to != s)
            def _():
                send(srcs[j], out.at[y], (i, to), n)

            @pl.when(to == s)
            def _():
                keep(srcs[j], out.at[y], n)

    give_back([q.xout.at[j] for j in range(z.ny)], q.lat_out, n_lo)
    give_back([q.gxo.at[j] for j in range(z.ny)], q.glat_out, n_go)
    media_back(0)
    norms_pair()
    h = z.pm // 2
    q.msend[...] = q.macc[at16((1 - c) * h, h)].astype(z.mt)
    send(q.msend, q.mrecv, sib, n_md)
    grads_second(0)
    for l in range(1, L):
        grads_last(l)
    norms_spread()
    arrive(q.mrecv, n_md)
    sent(q.mrecv, n_md)
    xhat, rstd = centre(q.media[pl.ds(c * z.ny, z.ny)].astype(F32).reshape(h, z.d))
    gm = pull(xhat, rstd, q.macc[at16(c * h, h)] + q.mrecv[...].astype(F32), jnp.ones((1, z.d), F32))
    mo = q.mn.at[0] if z.mt == BF else q.cm
    for j in range(z.ny):
        mo[j * z.pr:(j + 1) * z.pr] = gm[j * z.pr:(j + 1) * z.pr].astype(z.mt)
    srcs = [mo.at[pl.ds(j * z.pr, z.pr)] for j in range(z.ny)]
    give_back(srcs, q.gmedia_out, n_mo)
    grads_third(0)
    for l in range(1, L):
        grads_out(l)
        ff_out(l)
    ff_out(0)
    norms_out()
    grads_last(0)
    grads_out(0)
    arrive(q.lat_out, n_lo)
    arrive(q.glat_out, n_go)
    arrive(q.gmedia_out, n_mo)
    rows_sent()
    for j in range(z.ny):
        @pl.when(c * z.ny + j != s)
        def _():
            gone(q.xout.at[0], n_lo)
            gone(q.gxo.at[0], n_go)
            gone(srcs[0], n_mo)
    if z.fused:
        part = q.nrecv.at[pl.ds(0, z.ni - 1)]
        rest = q.nrecv.at[0, pl.ds(0, z.ns - 1)]
        gone(part, n_nrm)
        gone(rest, n_nrm)
    for ref, n in waits:
        gone(ref, n)


def call(z, *args):
    ins, outs, scratch = inputs_of(z), outputs_of(z), scratch_of(z)
    names = [n for n, _ in ins] + list(outs) + list(scratch)
    got = pl.pallas_call(
        functools.partial(kernel, z, names),
        out_shape=[jax.ShapeDtypeStruct(s, d) for _, s, d in outs.values()],
        in_specs=[pl.BlockSpec(memory_space=m) for _, m in ins],
        out_specs=[pl.BlockSpec(memory_space=m) for m, _, _ in outs.values()],
        scratch_shapes=list(scratch.values()),
        compiler_params=pltpu.CompilerParams(collective_id=0, has_side_effects=True, vmem_limit_bytes=62 * 2**20),
    )(*args)
    return types.SimpleNamespace(**dict(zip(outs, got)))


def body(mesh, media, latents, counts, wq, wkv, wout, wup, wdown, norms, cotangent):
    z = Sizes(mesh, media, latents, wq, wkv, wout, wup, wdown)
    L, D, H = z.layers, z.d, z.half
    i, s = lax.axis_index("img"), lax.axis_index("seq")
    y, c = s // 2, s % 2
    k = i * z.ny + y
    pos = k % TP
    latcot = jnp.stack([latents, cotangent], axis=1).astype(z.lt)
    media = media.astype(z.mt)
    own = norms.reshape(6 * L, -1)
    if z.fused:
        width = own.shape[1]
        tile = jnp.zeros((16, z.lanes), own.dtype)
        tile = lax.dynamic_update_slice(tile, own, (0, s * width))
        o = call(z, media, latcot, counts, tile, wq, wkv, wout, wup, wdown)
        gn = lax.dynamic_slice(o.gn_out, (0, s * width), (6 * L, width)).reshape(L, 6, width)
        return (o.lat_out.astype(BF), o.gmedia_out.astype(F32), o.glat_out, o.gq_out, o.gkv_out, o.go_out,
                o.gup_out, o.gdn_out, gn)

    def pick(v, axis, index):
        return lax.dynamic_index_in_dim(v, index, axis, keepdims=False)

    def gather(v, axis):
        return lax.all_gather(v, BOTH, axis=axis, tiled=True)

    nrm = jnp.pad(gather(own, 1).astype(F32), ((0, 16 - 6 * L), (0, 0)))
    fq = pick(gather(wq, 1).reshape(L, D, 2, H), 2, c)
    fkv = pick(gather(wkv, 1).reshape(L, D, 2, 2, H), 3, c).reshape(L, D, 2 * H)
    wqkv = jnp.concatenate([fq, fkv], axis=2).reshape(L, *z.blk, z.qrows, 3 * H)
    wo = gather(wout, 1).reshape(L, *z.blk, 2, z.orows // 2, D)
    fup = pick(gather(wup, 1).reshape(L, D, z.dp, TP, z.fc), 3, pos).reshape(L, 1, 2, D // 2, z.fs)
    fdn = pick(gather(wdown, 1).reshape(L, z.dp, TP, z.fc, D), 2, pos).reshape(L, 1, 2, z.fs // 2, D)
    o = call(z, media, latcot, counts, nrm, wqkv, wo, fup, fdn)

    def spread(g, shape, axis, index):
        return lax.dynamic_update_index_in_dim(jnp.zeros(shape, F32), g.astype(F32), index, axis)

    def scatter(g):
        return lax.psum_scatter(g, BOTH, scatter_dimension=1, tiled=True)

    gat = o.gat_out.reshape(L, z.nblk, z.qrows, z.wide)
    gout = jnp.concatenate([gat[:, :, : z.orows, 3 * H :], gat[:, :, z.orows : 2 * z.orows, 3 * H :]], axis=3)
    gout = gout.reshape(L, z.inner, D // 2)
    gat = gat.reshape(L, D, z.wide)
    gq = scatter(spread(gat[:, :, :H], (L, D, 2, H), 2, c).reshape(L, D, z.inner))
    gkv = spread(gat[:, :, H : 3 * H].reshape(L, D, 2, H), (L, D, 2, 2, H), 3, c)
    gkv = scatter(gkv.reshape(L, D, 2 * z.inner))
    go = scatter(spread(gout, (L, z.inner, 2, D // 2), 2, c).reshape(L, z.inner, D))
    gu = spread(o.gup_out.reshape(L, D, z.dp, z.fc), (L, D, z.dp, TP, z.fc), 3, pos)
    gu = scatter(gu.reshape(L, D, z.ff))
    gd = spread(o.gdn_out.reshape(L, z.dp, z.fc, D), (L, z.dp, TP, z.fc, D), 2, pos)
    gd = scatter(gd.reshape(L, z.ff, D))
    gn = lax.psum_scatter(o.gn_out, BOTH, scatter_dimension=1, tiled=True)[: 6 * L].reshape(L, 6, -1)
    return o.lat_out.astype(BF), o.gmedia_out.astype(F32), o.glat_out, gq, gkv, go, gu, gd, gn


def solution(mesh):
    rows = P("img", "seq", None)
    weight = P(None, BOTH, None)
    return jax.shard_map(
        functools.partial(body, mesh),
        mesh=mesh,
        in_specs=(rows, rows, P("img"), weight, weight, weight, weight, weight, P(None, None, BOTH), rows),
        out_specs=(rows, rows, rows, weight, weight, weight, weight, weight, P(None, None, BOTH)),
        check_vma=False,
    )
```

```python
import functools
import types

import jax
import jax.numpy as jnp
from jax import lax
from jax.experimental import pallas as pl
from jax.experimental.pallas import tpu as pltpu
from jax.sharding import PartitionSpec as P

HEAD = 64
EPS = 1e-05
MESH = pl.DeviceIdType.MESH
BF = jnp.bfloat16
F32 = jnp.float32
TP = 8
BOTH = ("img", "seq")


class Sizes:
    def __init__(self, mesh, media, latents, wq, wkv, wout, wup, wdown):
        self.ni, self.ns = mesh.shape["img"], mesh.shape["seq"]
        self.ny = self.ns // 2
        self.chips = self.ni * self.ny
        self.layers = wq.shape[0]
        self.d = media.shape[2]
        self.nimg, self.pr = media.shape[0], media.shape[1]
        self.lr = latents.shape[1]
        self.inner = wq.shape[2]
        self.half = self.inner // 2
        self.ff = wup.shape[2]
        self.fs = self.ff // TP
        self.dp = self.chips // TP
        self.fc = self.ff // self.chips
        self.pm = self.pr * self.ns
        self.latn = self.lr * self.ns
        self.r = self.latn // 2
        self.keys = self.pm + self.latn
        self.heads = self.half // HEAD
        self.rows = TP * self.r
        self.mt = BF if self.pr % 16 == 0 else F32
        self.lt = BF if self.lr % 16 == 0 else F32
        self.rq, self.ro, self.rd = wq.shape[1], wout.shape[1], wdown.shape[1]
        self.lanes = self.d // self.ni
        whole_tiles = all(v % 16 == 0 for v in (self.rq, self.ro, self.rd))
        whole_tiles = whole_tiles and self.fc % 128 == 0 and self.lanes % 128 == 0
        self.fused = whole_tiles and self.ny == 2 == self.layers and self.ni % 4 == 0
        self.blk = (self.ni // 2, 2, self.ny) if self.fused else (2, 1, 1)
        self.nblk = self.blk[0] * self.blk[1] * self.blk[2]
        self.qrows = self.d // self.nblk
        self.orows = self.inner // self.nblk
        self.quart = self.d // 4
        assert self.nimg == self.ny and TP % self.ny == 0


def dot(a, b, ca=1, cb=0):
    return lax.dot_general(a, b, (((ca,), (cb,)), ((), ())), preferred_element_type=F32)


def centre(v):
    c = v - jnp.mean(v, axis=-1, keepdims=True)
    rstd = lax.rsqrt(jnp.mean(c * c, axis=-1, keepdims=True) + EPS)
    return c * rstd, rstd


def pull(xhat, rstd, cot, gain):
    g = cot * gain
    m1 = jnp.mean(g, axis=-1, keepdims=True)
    m2 = jnp.mean(g * xhat, axis=-1, keepdims=True)
    return rstd * (g - m1 - xhat * m2)


def col_sum(v):
    return jnp.sum(v, axis=0, keepdims=True)


def inputs_of(z):
    names = ["media_in", "lat_in", "cot_in", "counts", "nrm_in"]
    if z.fused:
        names += ["wq_in", "wkv_in", "wo_in", "wup_in", "wdn_in"]
    else:
        names += ["wq_in", "wk_in", "wv_in", "wo_in", "wup_in", "wdn_in"]
    return [(n, pltpu.SMEM if n == "counts" else pl.ANY) for n in names]


def outputs_of(z):
    L, D = z.layers, z.d
    outs = dict(
        lat_out=((z.ny, z.lr, D), z.lt),
        gmedia_out=((z.ny, z.pr, D), z.mt),
        glat_out=((z.ny, z.lr, D), F32),
    )
    if z.fused:
        outs.update(
            qs_out=((L, 3, 2, z.rq, z.half), F32),
            os_out=((L, 2, 2, z.ro, z.quart), F32),
            upr=((L, z.chips, z.rq, z.fs), BF),
            dnr=((L, z.dp, z.rd, D), BF),
            gnr=((z.chips, 16, z.lanes), F32),
        )
    else:
        outs.update(
            gaq_out=((L, *z.blk, z.qrows, z.half), BF),
            gak_out=((L, *z.blk, z.qrows, z.half), BF),
            gav_out=((L, *z.blk, z.qrows, z.half), BF),
            gao_out=((L, *z.blk, 2 * z.orows, z.quart), BF),
            gup_out=((L, 1, 2, D // 2, z.fs), BF),
            gdn_out=((L, 1, 2, z.fs // 2, D), BF),
            gn_out=((16, D), F32),
        )
    return outs


def scratch_of(z):
    L, D, R, T = z.layers, z.d, z.r, TP
    kq = z.heads * z.latn
    cu = z.chips if z.fused else 1
    gd = z.dp if z.fused else 1
    v = dict(
        media=((z.ns, z.pr, D), z.mt),
        lc=((2, z.ny, z.lr, D), z.lt),
        mn=((L, z.keys, D), BF),
        kv=((L, z.keys, 2 * z.half), BF),
        wq=((L, *z.blk, z.qrows, z.half), BF),
        wk=((L, *z.blk, z.qrows, z.half), BF),
        wv=((L, *z.blk, z.qrows, z.half), BF),
        wo=((L, *z.blk, 2, z.orows // 2, D), BF),
        wup=((L, cu, 2, D // (2 * cu), z.fs), BF),
        wdn=((L, gd, 2, z.fs // (2 * gd), D), BF),
        nrm=((16, D), F32),
        q4=((L, kq, z.half), BF),
        pexp=((L, kq, z.keys), F32),
        rtot=((L, kq, 1), F32),
        att4=((L, z.latn, z.half), F32),
        atta=((L, 2, z.latn, z.half), BF),
        aft=((L, R, D), F32),
        ffa=((L, T, R, D), BF),
        hp=((L, z.rows, z.fs), F32),
        act=((L, z.rows, z.fs), BF),
        xs=((L, R, D), F32),
        gza=((L, T, R, D), BF),
        psend=((2 * L, T, R, D), BF),
        precv=((2 * L, T, R, D), BF),
        gpre=((L, z.rows, z.fs), BF),
        gya=((L, 2, R, D), BF),
        gl=((L, 2, R, D), F32),
        grecv=((L, R, D), F32),
        gkvm=((L, z.keys, 2 * z.half), BF),
        macc=((z.pm, D), F32),
        msend=((z.pm // 2, D), z.mt),
        mrecv=((z.pm // 2, D), z.mt),
        gn=((16, D), F32),
        xout=((z.ny, z.lr, D), z.lt),
        gxo=((z.ny, z.lr, D), F32),
        cm=((z.pm, D), F32),
        fold=((kq, z.half), F32),
        gak=((L, *z.blk, z.qrows, z.half), BF),
        gav=((L, *z.blk, z.qrows, z.half), BF),
        gaq=((L, *z.blk, z.qrows, z.half), BF),
        gao=((L, *z.blk, 2 * z.orows, z.quart), BF),
        gup=((L, cu, 2, D // (2 * cu), z.fs), BF),
        gdn=((L, gd, 2, z.fs // (2 * gd), D), BF),
    )
    if z.fused:
        za = z.blk[0]
        v.update(
            ntile=((16, z.lanes), BF),
            npair=((16, z.lanes), BF),
            nrecv=((z.chips, 16, z.lanes), BF),
            updr=((L, z.chips, z.rq, z.fs), BF),
            ups=((L, z.chips, z.rq, z.fs), BF),
            dndr=((L, z.dp, z.rd, D), BF),
            dns=((L, z.dp, z.rd, D), BF),
            gns=((16, D), F32),
            gnd=((16, D), F32),
        )
        for part in "kvqo":
            rows, cols = (2 * z.orows, z.quart) if part == "o" else (z.qrows, z.half)
            v["ra" + part] = ((L, za, 2, rows, cols), BF)
            v["sa" + part] = ((L, za, 2, rows, cols), BF)
            v["rb" + part] = ((L, za, rows, cols), BF)
            v["sb" + part] = ((L, za, rows, cols), BF)
            v["rc" + part] = ((L, za, rows, cols), BF)
            v["sf" + part] = ((L, rows, cols), F32)
    out = {n: pltpu.VMEM(s, d) for n, (s, d) in v.items()}
    out.update(ss=pltpu.SemaphoreType.DMA((NSEM,)), rs=pltpu.SemaphoreType.DMA((NSEM,)), ls=pltpu.SemaphoreType.DMA((32,)))
    return out


NSEM = 160


def kernel(z, names, *refs):
    L = z.layers
    q = types.SimpleNamespace(**dict(zip(names, refs)))
    ss, rs, ls = q.ss, q.rs, q.ls
    i = lax.axis_index("img")
    s = lax.axis_index("seq")
    y, c = s // 2, s % 2
    k = i * z.ny + y
    pos, grp = k % TP, k // TP
    sib = (i, y * 2 + (1 - c))
    a, b = i // 2, i % 2

    def chip(kk, cc):
        return (kk // z.ny, (kk % z.ny) * 2 + cc)

    def peer(t):
        return chip(grp * TP + (pos + t) % TP, c)

    waits = []
    used = [0]

    def sem():
        used[0] += 1
        return used[0] - 1

    def send(src, dst, dev, n):
        pltpu.make_async_remote_copy(src, dst, ss.at[n], rs.at[n], device_id=dev, device_id_type=MESH).start()

    def send_by_core(src0, dst0, src1, dst1, dev, n):
        @pl.when(c == 0)
        def _():
            send(src0, dst0, dev, n)

        @pl.when(c == 1)
        def _():
            send(src1, dst1, dev, n)

    def keep(src, dst, n):
        pltpu.make_async_copy(src, dst, rs.at[n]).start()

    def arrive(ref, n):
        pltpu.make_async_copy(ref, ref, rs.at[n]).wait()

    def gone(ref, n):
        pltpu.make_async_copy(ref, ref, ss.at[n]).wait()

    def sent(ref, n):
        waits.append((ref, n))

    bar = pltpu.get_barrier_semaphore()

    def greet(dev):
        pl.semaphore_signal(bar, inc=1, device_id=dev, device_id_type=MESH)

    def greet_chip(t, _):
        greet(chip((k + t) % z.chips, c))
        return 0

    greet(sib)
    for t in range(1, z.ny):
        greet((i, ((y + t) % z.ny) * 2 + (1 - c)))
    lax.fori_loop(1, z.chips, greet_chip, 0)
    pl.semaphore_wait(bar, z.chips - 1 + z.ny)

    def lanes(start, size):
        return pl.ds(pl.multiple_of(start, 128), size)

    def at16(start, size):
        return pl.ds(pl.multiple_of(start, 16), size)

    H = z.half
    if z.fused:
        za = z.blk[0]
        n_w0, n_w1, n_w2, n_w3 = ({p: [sem() for _ in range(L)] for p in "kvqo"} for _ in range(4))
        n_od = [sem() for _ in range(L)]
        n_ua, n_ub, n_da, n_db = ([sem() for _ in range(L)] for _ in range(4))
        n_np, n_nrm = sem(), sem()
        xdev = (i + 1 - 2 * b, s)
        ydev = (i, (1 - y) * 2 + c)
        first = (xdev[0] * (1 - c) + i * c, s * (1 - c) + ydev[1] * c)
        second = (i * (1 - c) + xdev[0] * c, ydev[1] * (1 - c) + s * c)
        bufs = dict(k=q.wk, v=q.wv, q=q.wq)

        def block(p, l, *at):
            if p == "o":
                return q.wo.at[(l, *at, *(slice(None),) * (3 - len(at)), c)]
            return bufs[p].at[(l, *at)]

        def weights_pair(l):
            rows = at16(c * z.rq, z.rq)
            for cc, dev in ((1 - c, sib), (c, None)):
                for p, src in (
                    ("k", q.wkv_in.at[l, :, lanes(cc * H, H)]),
                    ("v", q.wkv_in.at[l, :, lanes(z.inner + cc * H, H)]),
                    ("q", q.wq_in.at[l, :, lanes(cc * H, H)]),
                ):
                    dst = bufs[p].at[l, a, b, y, rows]
                    if dev is None:
                        keep(src, dst, n_w0[p][l])
                    else:
                        send(src, dst, dev, n_w0[p][l])
            for p in "kvq":
                sent(q.wq.at[l, 0, 0, 0, pl.ds(0, z.rq)], n_w0[p][l])
            keep(q.wo_in.at[l], q.wo.at[l, a, b, y, c], n_w0["o"][l])

        def weights_z(l, parts):
            for p in parts:
                own = block(p, l, a, b, y)
                arrive(own, n_w0[p][l])
                for t in range(1, za):
                    send(own, own, (((a + t) % za) * 2 + b, s), n_w1[p][l])

        def weights_first(l, parts):
            for p in parts:
                got = block(p, l, pl.ds(0, za - 1), 0, 0)
                arrive(got, n_w1[p][l])
                sent(got, n_w1[p][l])
                own = block(p, l, slice(None), b, y)
                send(own, own, first, n_w2[p][l])

        def weights_second(l, parts):
            for p in parts:
                got = block(p, l, slice(None), 0, 0)
                arrive(got, n_w2[p][l])
                sent(got, n_w2[p][l])
                ref0, ref1 = block(p, l, slice(None), slice(None), y), block(p, l, slice(None), b)
                send_by_core(ref0, ref0, ref1, ref1, second, n_w3[p][l])

        def weights_end(l, parts):
            for p in parts:
                got = block(p, l, slice(None), 0)
                arrive(got, n_w3[p][l])
                sent(got, n_w3[p][l])
                if p == "o":
                    ref = block(p, l)
                    send(ref, ref, sib, n_od[l])

        def weights_out_end(l):
            ref = q.wo.at[l, :, :, :, 0]
            arrive(ref, n_od[l])
            sent(ref, n_od[l])

        def weights_ff(l):
            def one(t, _):
                kk = (k + t) % z.chips
                dev = chip(kk, c)
                for g in range(z.dp):
                    src = q.wup_in.at[l, :, lanes((g * TP + kk % TP) * z.fc, z.fc)]
                    send(src, q.wup.at[l, k, c, :, pl.ds(g * z.fc, z.fc)], dev, n_ua[l])
                return 0

            for g in range(1, z.dp):
                dev = chip(((grp + g) % z.dp) * TP + pos, c)
                send(q.wdn_in.at[l], q.wdn.at[l, grp, c], dev, n_da[l])
            keep(q.wdn_in.at[l], q.wdn.at[l, grp, c], n_da[l])
            lax.fori_loop(1, z.chips, one, 0)
            for g in range(z.dp):
                src = q.wup_in.at[l, :, lanes((g * TP + pos) * z.fc, z.fc)]
                keep(src, q.wup.at[l, k, c, :, pl.ds(g * z.fc, z.fc)], n_ua[l])
            sent(q.wup.at[l, pl.ds(0, z.chips - 1), 0], n_ua[l])
            sent(q.wdn.at[l, pl.ds(0, z.dp - 1), 0], n_da[l])

        def weights_ff_share(l):
            arrive(q.wup.at[l, :, 0], n_ua[l])
            send(q.wup.at[l, :, c], q.wup.at[l, :, c], sib, n_ub[l])
            arrive(q.wdn.at[l, :, 0], n_da[l])
            send(q.wdn.at[l, :, c], q.wdn.at[l, :, c], sib, n_db[l])

        def weights_ff_end(l):
            arrive(q.wup.at[l, :, 0], n_ub[l])
            sent(q.wup.at[l, :, 0], n_ub[l])
            arrive(q.wdn.at[l, :, 0], n_db[l])
            sent(q.wdn.at[l, :, 0], n_db[l])

        def norms_start():
            send(q.nrm_in, q.ntile, sib, n_np)
            pltpu.make_async_copy(q.nrm_in, q.npair, ls.at[0]).start()

        def norms_spread_in():
            pltpu.make_async_copy(q.nrm_in, q.npair, ls.at[0]).wait()
            arrive(q.ntile, n_np)
            sent(q.ntile, n_np)
            q.nrecv[k] = q.npair[...] + q.ntile[...]

            def one(t, _):
                send(q.nrecv.at[k], q.nrecv.at[k], chip((k + t) % z.chips, c), n_nrm)
                return 0

            lax.fori_loop(1, z.chips, one, 0)

        def norms_end():
            part = q.nrecv.at[pl.ds(0, z.chips - 1)]
            arrive(part, n_nrm)
            sent(part, n_nrm)
            for ii in range(z.ni):
                v = q.nrecv[ii * z.ny].astype(F32)
                for j in range(1, z.ny):
                    v = v + q.nrecv[ii * z.ny + j].astype(F32)
                q.nrm[:, ii * z.lanes:(ii + 1) * z.lanes] = v
    else:
        loads = [(q.nrm_in, q.nrm)]
        for l in range(L):
            loads += [(getattr(q, n + "_in").at[l], getattr(q, n).at[l]) for n in ("wk", "wq", "wo", "wup", "wdn", "wv")]

        def norms_start():
            for n, (src, dst) in enumerate(loads):
                pltpu.make_async_copy(src, dst, ls.at[n]).start()

        def load_end(n):
            pltpu.make_async_copy(*loads[n], ls.at[n]).wait()

        def norms_spread_in():
            pass

        def norms_end():
            load_end(0)

        def nothing(l, parts=None):
            pass

        weights_pair = weights_z = weights_first = weights_second = nothing
        weights_ff = weights_ff_share = nothing

        def weights_end(l, parts):
            for p in parts:
                if p != "o":
                    load_end(1 + 6 * l + dict(k=0, q=1, v=5)[p])

        def weights_out_end(l):
            load_end(3 + 6 * l)

        def weights_ff_end(l):
            load_end(4 + 6 * l)
            load_end(5 + 6 * l)

    def w_q(l):
        return q.wq[l].reshape(z.d, H)

    def w_k(l):
        return q.wk[l].reshape(z.d, H)

    def w_v(l):
        return q.wv[l].reshape(z.d, H)

    def w_up(l):
        return q.wup[l].reshape(z.d, z.fs)

    def w_dn(l):
        return q.wdn[l].reshape(z.fs, z.d)

    n_la, n_lb, n_ma, n_mb = sem(), sem(), sem(), sem()
    n_ff, n_gz, n_ln, n_at, n_gy, n_gl = ([sem() for _ in range(L)] for _ in range(6))
    n_rs = [sem() for _ in range(2 * L)]
    n_md, n_lo, n_go, n_mo = sem(), sem(), sem(), sem()
    own_slot = s % z.ny

    def rows_start():
        for t in range(1, z.ny):
            yy = (y + t) % z.ny
            send(q.media_in.at[yy], q.media.at[s], (i, yy * 2 + c), n_ma)
        keep(q.media_in.at[y], q.media.at[s], n_ma)
        send(q.media_in.at[y], q.media.at[s], sib, n_mb)
        for yy in range(z.ny):
            to = yy * 2 + s // z.ny

            @pl.when(to != s)
            def _():
                send(q.lat_in.at[yy], q.lc.at[0, own_slot], (i, to), n_la)
                send(q.cot_in.at[yy], q.lc.at[1, own_slot], (i, to), n_lb)

            @pl.when(to == s)
            def _():
                keep(q.lat_in.at[yy], q.lc.at[0, own_slot], n_la)
                keep(q.cot_in.at[yy], q.lc.at[1, own_slot], n_lb)

    def media_share():
        arrive(q.media.at[pl.ds(0, z.ny)], n_ma)
        for t in range(1, z.ny):
            yy = (y + t) % z.ny
            send(q.media.at[yy * 2 + c], q.media.at[yy * 2 + c], sib, n_mb)

    def rows_sent():
        for yy in range(z.ny):
            @pl.when(yy * 2 + s // z.ny != s)
            def _():
                gone(q.lc.at[0, 0], n_la)
                gone(q.lc.at[0, 0], n_lb)
        if z.ny > 1:
            gone(q.media.at[pl.ds(0, z.ny - 1)], n_ma)
        gone(q.media.at[pl.ds(0, z.ny)], n_mb)

    def gather_start(buf, value, n):
        buf[pos] = value
        for t in range(1, TP):
            send(buf.at[pos], buf.at[pos], peer(t), n)

    def gather_end(buf, n):
        arrive(buf.at[pl.ds(0, TP - 1)], n)
        sent(buf.at[pl.ds(0, TP - 1)], n)

    def swap(ref, value, n):
        ref[...] = value
        send(ref, ref, sib, n)
        arrive(ref, n)
        sent(ref, n)

    def scatter_put(part, j):
        q.psend[j] = part.astype(BF).reshape(TP, z.r, z.d)

    def scatter_start(j):
        for t in range(1, TP):
            o = (pos + t) % TP
            send(q.psend.at[j, o], q.precv.at[j, pos], peer(t), n_rs[j])
        q.precv[j, pos] = q.psend[j, pos]

    def scatter_end(j):
        arrive(q.precv.at[j, pl.ds(0, TP - 1)], n_rs[j])
        sent(q.precv.at[j, pl.ds(0, TP - 1)], n_rs[j])
        out = q.precv[j, 0].astype(F32)
        for t in range(1, TP):
            out = out + q.precv[j, t].astype(F32)
        return out

    def vec(l, m):
        return q.nrm[6 * l + m][None, :]

    lane_head = lax.broadcasted_iota(jnp.int32, (1, H), 1) // HEAD

    def stack_heads(v):
        return jnp.concatenate([jnp.where(lane_head == h, v, jnp.zeros_like(v)) for h in range(z.heads)], axis=0)

    def fold_heads(v):
        out = None
        q.fold[...] = v
        for h in range(z.heads):
            part = jnp.where(lane_head == h, q.fold[h * z.latn:(h + 1) * z.latn], 0.0)
            out = part if out is None else out + part
        return out

    key_pos = lax.broadcasted_iota(jnp.int32, (1, z.keys), 1)
    live = (key_pos < q.counts[y]) | (key_pos >= z.pm)

    def norm_piece(j, _):
        xhat, _ = centre(q.media[j].astype(F32))
        rows = pl.ds(pl.multiple_of(j * z.pr, 8), z.pr)
        for l in range(L):
            q.mn[l, rows] = (xhat * vec(l, 0) + vec(l, 1)).astype(BF)
        return 0

    def media_kv(l):
        weights_end(l, "k")
        q.kv[l, :z.pm, :H] = dot(q.mn[l, :z.pm], w_k(l)).astype(BF)
        weights_end(l, "v")
        q.kv[l, :z.pm, H:] = dot(q.mn[l, :z.pm], w_v(l)).astype(BF)

    def attention(l):
        xhat, _ = centre(q.xs[l])
        swap(q.mn.at[l, at16(z.pm + c * z.r, z.r)], (xhat * vec(l, 2) + vec(l, 3)).astype(BF), n_ln[l])
        q.kv[l, z.pm:, :H] = dot(q.mn[l, z.pm:], w_k(l)).astype(BF)
        q.kv[l, z.pm:, H:] = dot(q.mn[l, z.pm:], w_v(l)).astype(BF)
        weights_end(l, "q")
        queries = stack_heads(dot(q.mn[l, z.pm:], w_q(l)).astype(BF))
        q.q4[l] = queries
        scores = dot(queries, q.kv[l, :, :H], 1, 1) * 0.125
        scores = jnp.where(live, scores, -1000000000.0)
        e = jnp.exp(scores - jnp.max(scores, axis=-1, keepdims=True))
        rt = jnp.sum(e, axis=-1, keepdims=True)
        q.pexp[l] = e
        q.rtot[l] = rt

    def attention_mix(l):
        own = fold_heads(dot(q.pexp[l].astype(BF), q.kv[l, :, H:]) / q.rtot[l])
        q.att4[l] = own
        swap(q.atta.at[l, c], own.astype(BF), n_at[l])

    def attention_out(l):
        mine = at16(c * z.r, z.r)
        att = jnp.concatenate([q.atta[l, 0, mine], q.atta[l, 1, mine]], axis=1)
        after = q.xs[l] + dot(att, q.wo[l].reshape(z.inner, z.d))
        q.aft[l] = after
        xhat, _ = centre(after)
        gather_start(q.ffa.at[l], (xhat * vec(l, 4) + vec(l, 5)).astype(BF), n_ff[l])

    def hidden(l):
        h = dot(q.ffa[l].reshape(z.rows, z.d), w_up(l))
        q.hp[l] = h
        q.act[l] = (h * (0.5 * (1.0 + lax.erf(h * 0.7071067811865476)))).astype(BF)

    def down(l):
        scatter_put(dot(q.act[l], w_dn(l)), l)

    def ff_back(l):
        g = dot(q.gza[l].reshape(z.rows, z.d), w_dn(l), 1, 1)
        h = q.hp[l]
        slope = 0.5 * (1.0 + lax.erf(h * 0.7071067811865476)) + h * 0.3989422804014327 * jnp.exp(-0.5 * h * h)
        q.gpre[l] = (g * slope).astype(BF)
        scatter_put(dot(q.gpre[l], w_up(l), 1, 1), L + l)
        scatter_start(L + l)

    def ff_grads(l):
        q.gdn[l] = dot(q.act[l], q.gza[l].reshape(z.rows, z.d), 0, 0).astype(BF).reshape(q.gdn.shape[1:])
        q.gup[l] = dot(q.ffa[l].reshape(z.rows, z.d), q.gpre[l], 0, 0).astype(BF).reshape(q.gup.shape[1:])

    def attn_back(l, gx):
        gff = scatter_end(L + l)
        xhat, rstd = centre(q.aft[l])
        q.gn[6 * l + 4] = jnp.sum(gff * xhat, axis=0)
        q.gn[6 * l + 5] = jnp.sum(gff, axis=0)
        gafter = gx + pull(xhat, rstd, gff, vec(l, 4))
        swap(q.gya.at[l, c], gafter.astype(BF), n_gy[l])
        out_grads(l)
        grads_first(l, "o")
        return gafter

    def attn_back_end(l, gafter):
        gy = q.gya[l].reshape(z.latn, z.d)
        hb = z.blk[0] // 2
        wo_own = q.wo[l, pl.ds(c * hb, hb)].reshape(H, z.d)
        gatt = dot(gy, wo_own, 1, 1).astype(BF)
        g4 = stack_heads(gatt.astype(F32))
        delta = jnp.sum(g4 * stack_heads(q.att4[l]), axis=-1, keepdims=True)
        rt = q.rtot[l]
        e = q.pexp[l]
        gp = dot(g4.astype(BF), q.kv[l, :, H:], 1, 1)
        gs = (e / rt * (gp - delta)).astype(BF)
        gq = (fold_heads(dot(gs, q.kv[l, :, :H])) * 0.125).astype(BF)
        gk = (dot(gs, q.q4[l], 0, 0) * 0.125).astype(BF)
        gv = dot(e.astype(BF), (g4 / rt).astype(BF), 0, 0).astype(BF)
        glat = jnp.concatenate([gq, gk[z.pm:], gv[z.pm:]], axis=1)
        w = jnp.concatenate([w_q(l), w_k(l), w_v(l)], axis=1)
        q.gl[l] = dot(glat, w, 1, 1).reshape(2, z.r, z.d)
        send(q.gl.at[l, 1 - c], q.grecv.at[l], sib, n_gl[l])
        q.gkvm[l, :, :H] = gk
        q.gkvm[l, :, H:] = gv
        arrive(q.grecv.at[l], n_gl[l])
        sent(q.grecv.at[l], n_gl[l])
        gln = q.gl[l, c] + q.grecv[l]
        xhat, rstd = centre(q.xs[l])
        q.gn[6 * l + 2] = jnp.sum(gln * xhat, axis=0)
        q.gn[6 * l + 3] = jnp.sum(gln, axis=0)
        return gafter + pull(xhat, rstd, gln, vec(l, 2)), gq

    def out_grads(l):
        att = jnp.concatenate([q.atta[l, 0], q.atta[l, 1]], axis=1)
        cols = lanes(c * (z.d // 2), z.d // 2)
        gyc = jnp.concatenate([q.gya[l, 0, :, cols], q.gya[l, 1, :, cols]], axis=0)
        g = dot(att, gyc, 0, 0).astype(BF).reshape(*z.blk, z.orows, z.d // 2)
        q.gao[l, :, :, :, :z.orows] = g[..., :z.quart]
        q.gao[l, :, :, :, z.orows:] = g[..., z.quart:]

    def qkv_grads(l, gq, p):
        shape = (*z.blk, z.qrows, H)
        if p == "q":
            q.gaq[l] = dot(q.mn[l, z.pm:], gq, 0, 0).astype(BF).reshape(shape)
        elif p == "k":
            q.gak[l] = dot(q.mn[l], q.gkvm[l, :, :H], 0, 0).astype(BF).reshape(shape)
        else:
            q.gav[l] = dot(q.mn[l], q.gkvm[l, :, H:], 0, 0).astype(BF).reshape(shape)

    def media_back(l):
        q.cm[...] = dot(q.gkvm[l, :z.pm], jnp.concatenate([w_k(l), w_v(l)], axis=1), 1, 1)

        def piece(j, sums):
            rows = pl.ds(pl.multiple_of(j * z.pr, 8), z.pr)
            xhat, rstd = centre(q.media[j].astype(F32))
            cotm = q.cm[rows]
            add = cotm * vec(l, 0)
            q.macc[rows] = add if l == L - 1 else q.macc[rows] + add
            return sums[0] + col_sum(cotm * xhat), sums[1] + col_sum(cotm)

        zero = jnp.zeros((1, z.d), F32)
        u, v = lax.fori_loop(0, z.ns, piece, (zero, zero))
        q.gn[6 * l + 0] = u[0]
        q.gn[6 * l + 1] = v[0]

    if z.fused:
        n_ra, n_rb, n_rc, n_rf = ({p: [sem() for _ in range(L)] for p in "kvqo"} for _ in range(4))
        n_ud, n_us, n_dd, n_ds = ([sem() for _ in range(L)] for _ in range(4))
        n_nd, n_ns = sem(), sem()

        def add_to(dst, x, w):
            dst[...] = (x[...].astype(F32) + w[...].astype(F32)).astype(BF)

        def at(name, l):
            return getattr(q, name).at[l]

        def grads_first(l, p):
            g, ra = at("ga" + p, l), at("ra" + p, l)
            send_by_core(g.at[:, :, 1 - y], ra, g.at[:, 1 - b], ra, second, n_ra[p][l])

        def grads_second(l, p):
            g, ra, sa, rb = at("ga" + p, l), at("ra" + p, l), at("sa" + p, l), at("rb" + p, l)
            arrive(ra, n_ra[p][l])
            sent(ra, n_ra[p][l])

            @pl.when(c == 0)
            def _():
                add_to(sa, g.at[:, :, y], ra)

            @pl.when(c == 1)
            def _():
                add_to(sa, g.at[:, b], ra)

            send_by_core(sa.at[:, 1 - b], rb, sa.at[:, 1 - y], rb, first, n_rb[p][l])

        def grads_third(l, p):
            sa, rb, sb, rc = at("sa" + p, l), at("rb" + p, l), at("sb" + p, l), at("rc" + p, l)
            arrive(rb, n_rb[p][l])
            sent(rb, n_rb[p][l])
            add_to(sb, sa.at[:, b * (1 - c) + y * c], rb)
            for t in range(1, za):
                o = (a + t) % za
                send(sb.at[o], rc.at[a], (o * 2 + b, s), n_rc[p][l])
            rc[a] = sb[a]

        def grads_last(l, p):
            rc, sf = at("rc" + p, l), at("sf" + p, l)
            part = rc.at[pl.ds(0, za - 1)]
            arrive(part, n_rc[p][l])
            sent(part, n_rc[p][l])
            v = rc[0].astype(F32)
            for t in range(1, za):
                v = v + rc[t].astype(F32)
            sf[...] = v
            if p != "o":
                mine, other = sf.at[at16(c * z.rq, z.rq)], sf.at[at16((1 - c) * z.rq, z.rq)]
                out = q.qs_out.at[l, "qkv".index(p), c]
                keep(mine, out, n_rf[p][l])
                send(other, out, sib, n_rf[p][l])
            else:
                for h in range(2):
                    mine, other = (sf.at[at16(h * z.orows + cc * z.ro, z.ro)] for cc in (c, 1 - c))
                    keep(mine, q.os_out.at[l, c, h], n_rf[p][l])
                    send(other, q.os_out.at[l, c, h], sib, n_rf[p][l])

        def grads_out(l, p):
            out = q.os_out.at[l] if p == "o" else q.qs_out.at[l, "qkv".index(p)]
            arrive(out, n_rf[p][l])
            sent(out.at[0], n_rf[p][l])

        def ff_pair(l):
            send(q.gup.at[l, :, 1 - c], q.updr.at[l], sib, n_ud[l])
            send(q.gdn.at[l, :, 1 - c], q.dndr.at[l], sib, n_dd[l])

        def ff_spread(l):
            arrive(q.dndr.at[l], n_dd[l])
            sent(q.dndr.at[l], n_dd[l])
            add_to(q.dns.at[l], q.gdn.at[l, :, c], q.dndr.at[l])
            for g in range(1, z.dp):
                o = (grp + g) % z.dp
                send(q.dns.at[l, o], q.dnr.at[l, grp], chip(o * TP + pos, c), n_ds[l])
            arrive(q.updr.at[l], n_ud[l])
            sent(q.updr.at[l], n_ud[l])
            add_to(q.ups.at[l], q.gup.at[l, :, c], q.updr.at[l])

            def one(t, _):
                kk = (k + t) % z.chips
                send(q.ups.at[l, kk], q.upr.at[l, k], chip(kk, c), n_us[l])
                return 0

            lax.fori_loop(1, z.chips, one, 0)
            keep(q.dns.at[l, grp], q.dnr.at[l, grp], n_ds[l])
            keep(q.ups.at[l, k], q.upr.at[l, k], n_us[l])

        def ff_out(l):
            arrive(q.dnr.at[l], n_ds[l])
            sent(q.dns.at[l, pl.ds(0, z.dp - 1)], n_ds[l])
            arrive(q.upr.at[l], n_us[l])
            sent(q.ups.at[l, pl.ds(0, z.chips - 1)], n_us[l])

        def norms_pair():
            send(q.gn, q.gnd, sib, n_nd)

        def norms_spread():
            arrive(q.gnd, n_nd)
            sent(q.gnd, n_nd)
            q.gns[...] = q.gn[...] + q.gnd[...]

            def one(t, _):
                kk = (k + t) % z.chips
                dev = chip(kk, c)
                send(q.gns.at[:, lanes(dev[0] * z.lanes, z.lanes)], q.gnr.at[k], dev, n_ns)
                return 0

            lax.fori_loop(1, z.chips, one, 0)
            keep(q.gns.at[:, lanes(i * z.lanes, z.lanes)], q.gnr.at[k], n_ns)

        def norms_out():
            arrive(q.gnr, n_ns)
            sent(q.gnr.at[pl.ds(0, z.chips - 1)], n_ns)
    else:
        def grads_first(l, p):
            n = 11 + "kvqo".index(p) * L + l
            pltpu.make_async_copy(getattr(q, "ga" + p).at[l], getattr(q, f"ga{p}_out").at[l], ls.at[n]).start()

        def grads_out(l, p):
            n = 11 + "kvqo".index(p) * L + l
            pltpu.make_async_copy(getattr(q, "ga" + p).at[l], getattr(q, f"ga{p}_out").at[l], ls.at[n]).wait()

        def ff_pair(l):
            pltpu.make_async_copy(q.gup.at[l], q.gup_out.at[l], ls.at[19 + l]).start()
            pltpu.make_async_copy(q.gdn.at[l], q.gdn_out.at[l], ls.at[21 + l]).start()

        def ff_out(l):
            pltpu.make_async_copy(q.gup.at[l], q.gup_out.at[l], ls.at[19 + l]).wait()
            pltpu.make_async_copy(q.gdn.at[l], q.gdn_out.at[l], ls.at[21 + l]).wait()

        grads_second = grads_third = grads_last = ff_spread = nothing

        def norms_pair():
            pass

        def norms_spread():
            pass

        def norms_out():
            pltpu.make_async_copy(q.gn, q.gn_out, ls.at[23]).start()
            pltpu.make_async_copy(q.gn, q.gn_out, ls.at[23]).wait()

    weights_pair(0)
    norms_start()
    rows_start()
    weights_z(0, "k")
    weights_z(0, "v")
    weights_z(0, "q")
    weights_z(0, "o")
    norms_spread_in()
    for l in range(1, L):
        weights_pair(l)
    weights_first(0, "k")
    arrive(q.lc.at[0], n_la)
    q.xs[0] = q.lc[0].astype(F32).reshape(z.r, z.d)
    media_share()
    weights_first(0, "v")
    norms_end()
    weights_second(0, "k")
    weights_first(0, "q")
    arrive(q.media.at[pl.ds(0, z.ny)], n_mb)
    weights_second(0, "v")
    weights_first(0, "o")
    for l in range(1, L):
        weights_z(l, "kvqo")
    weights_ff(0)
    lax.fori_loop(0, z.ns // 2, norm_piece, 0)
    weights_second(0, "q")
    lax.fori_loop(z.ns // 2, z.ns, norm_piece, 0)
    weights_second(0, "o")
    arrive(q.lc.at[1], n_lb)
    cot = q.lc[1].astype(F32).reshape(z.r, z.d)
    media_kv(0)
    for l in range(L):
        attention(l)
        if l + 1 < L:
            weights_first(l + 1, "kvqo")
        else:
            gather_start(q.gza.at[l], cot.astype(BF), n_gz[l])
        attention_mix(l)
        weights_end(l, "o")
        weights_out_end(l)
        attention_out(l)
        if l + 1 < L:
            weights_second(l + 1, "kvqo")
        weights_ff_share(l)
        weights_ff_end(l)
        if l + 1 < L:
            weights_ff(l + 1)
        gather_end(q.ffa.at[l], n_ff[l])
        hidden(l)
        if l + 1 < L:
            down(l)
            scatter_start(l)
            media_kv(l + 1)
            q.xs[l + 1] = q.aft[l] + scatter_end(l)
    gx = cot
    for l in reversed(range(L)):
        if l < L - 1:
            gather_start(q.gza.at[l], gx.astype(BF), n_gz[l])
            qkv_grads(l + 1, gq, "k")
            grads_first(l + 1, "k")
            grads_second(l + 1, "o")
            qkv_grads(l + 1, gq, "v")
            qkv_grads(l + 1, gq, "q")
            media_back(l + 1)
        gather_end(q.gza.at[l], n_gz[l])
        ff_back(l)
        if l < L - 1:
            grads_first(l + 1, "v")
            grads_first(l + 1, "q")
        ff_grads(l)
        ff_pair(l)
        if l < L - 1:
            grads_second(l + 1, "k")
            grads_third(l + 1, "o")
        else:
            down(l)
        ff_spread(l)
        gafter = attn_back(l, gx)
        if l < L - 1:
            grads_second(l + 1, "v")
            grads_second(l + 1, "q")
            grads_third(l + 1, "k")
        else:
            scatter_start(l)
        gx, gq = attn_back_end(l, gafter)
    qkv_grads(0, gq, "k")
    grads_first(0, "k")
    qkv_grads(0, gq, "v")
    grads_first(0, "v")
    qkv_grads(0, gq, "q")
    grads_first(0, "q")
    grads_second(0, "o")
    for l in range(1, L):
        grads_third(l, "v")
        grads_third(l, "q")
        grads_last(l, "o")
        grads_last(l, "k")
    q.gxo[...] = gx.reshape(z.ny, z.lr, z.d)
    q.xout[...] = (q.aft[L - 1] + scatter_end(L - 1)).astype(z.lt).reshape(z.ny, z.lr, z.d)

    def give_back(srcs, out, n):
        for j in range(z.ny):
            to = c * z.ny + j

            @pl.when(to != s)
            def _():
                send(srcs[j], out.at[y], (i, to), n)

            @pl.when(to == s)
            def _():
                keep(srcs[j], out.at[y], n)

    give_back([q.xout.at[j] for j in range(z.ny)], q.lat_out, n_lo)
    give_back([q.gxo.at[j] for j in range(z.ny)], q.glat_out, n_go)
    media_back(0)
    norms_pair()
    h = z.pm // 2
    q.msend[...] = q.macc[at16((1 - c) * h, h)].astype(z.mt)
    send(q.msend, q.mrecv, sib, n_md)
    grads_second(0, "k")
    grads_second(0, "v")
    grads_second(0, "q")
    grads_third(0, "o")
    norms_spread()
    arrive(q.mrecv, n_md)
    sent(q.mrecv, n_md)
    xhat, rstd = centre(q.media[pl.ds(c * z.ny, z.ny)].astype(F32).reshape(h, z.d))
    gm = pull(xhat, rstd, q.macc[at16(c * h, h)] + q.mrecv[...].astype(F32), jnp.ones((1, z.d), F32))
    mo = q.mn.at[0] if z.mt == BF else q.cm
    for j in range(z.ny):
        mo[j * z.pr:(j + 1) * z.pr] = gm[j * z.pr:(j + 1) * z.pr].astype(z.mt)
    srcs = [mo.at[pl.ds(j * z.pr, z.pr)] for j in range(z.ny)]
    give_back(srcs, q.gmedia_out, n_mo)
    grads_third(0, "k")
    grads_third(0, "v")
    grads_third(0, "q")
    for l in range(1, L):
        grads_last(l, "v")
        grads_last(l, "q")
    grads_last(0, "o")
    for l in range(1, L):
        grads_out(l, "o")
        grads_out(l, "k")
        grads_out(l, "v")
        grads_out(l, "q")
        ff_out(l)
    ff_out(0)
    norms_out()
    grads_last(0, "k")
    grads_last(0, "v")
    grads_last(0, "q")
    grads_out(0, "o")
    grads_out(0, "k")
    grads_out(0, "v")
    grads_out(0, "q")
    arrive(q.lat_out, n_lo)
    arrive(q.glat_out, n_go)
    arrive(q.gmedia_out, n_mo)
    rows_sent()
    for j in range(z.ny):
        @pl.when(c * z.ny + j != s)
        def _():
            gone(q.xout.at[0], n_lo)
            gone(q.gxo.at[0], n_go)
            gone(srcs[0], n_mo)
    for ref, n in waits:
        gone(ref, n)


def call(z, *args):
    ins, outs, scratch = inputs_of(z), outputs_of(z), scratch_of(z)
    names = [n for n, _ in ins] + list(outs) + list(scratch)
    got = pl.pallas_call(
        functools.partial(kernel, z, names),
        out_shape=[jax.ShapeDtypeStruct(s, d) for s, d in outs.values()],
        in_specs=[pl.BlockSpec(memory_space=m) for _, m in ins],
        out_specs=[pl.BlockSpec(memory_space=pl.ANY)] * len(outs),
        scratch_shapes=list(scratch.values()),
        compiler_params=pltpu.CompilerParams(collective_id=0, has_side_effects=True, vmem_limit_bytes=62 * 2**20),
    )(*args)
    return types.SimpleNamespace(**dict(zip(outs, got)))


def finish_kernel(z, lat_in, gm_in, gl_in, qs, os, upr, dnr, gnr, lat, gm, gl, gq, gkv, go, gup, gdn, gn):
    H = z.half
    lat[...] = lat_in[...]
    gm[...] = gm_in[...].astype(F32)
    gl[...] = gl_in[...]
    for cc in range(2):
        gq[0, :, cc * H:(cc + 1) * H] = qs[0, 0, cc]
        gkv[0, :, cc * H:(cc + 1) * H] = qs[0, 1, cc]
        gkv[0, :, z.inner + cc * H:z.inner + (cc + 1) * H] = qs[0, 2, cc]
        for h in range(2):
            col = cc * (z.d // 2) + h * z.quart
            go[0, :, col:col + z.quart] = os[0, cc, h]
    v = dnr[0, 0].astype(F32)
    for g in range(1, z.dp):
        v = v + dnr[0, g].astype(F32)
    gdn[0] = v
    for p in range(TP):
        v = upr[0, p].astype(F32)
        for g in range(1, z.dp):
            v = v + upr[0, g * TP + p].astype(F32)
        for g in range(z.dp):
            col = (g * TP + p) * z.fc
            gup[0, :, col:col + z.fc] = v[:, g * z.fc:(g + 1) * z.fc]
    s = lax.axis_index("seq")
    width = z.lanes // z.ns
    v = gnr[0]
    for t in range(1, z.chips):
        v = v + gnr[t]
    mine = v[:, :width]
    for j in range(1, z.ns):
        mine = jnp.where(s == j, v[:, j * width:(j + 1) * width], mine)
    for l in range(z.layers):
        gn[l] = mine[6 * l:6 * l + 6]


def finish(z, o):
    L, D = z.layers, z.d
    step = lambda *shape: pl.BlockSpec((1, *shape), lambda n: (n,) + (0,) * len(shape))
    whole = lambda *shape: pl.BlockSpec(shape, lambda n: (0,) * len(shape))
    width = z.lanes // z.ns
    outs = [
        ((z.ny, z.lr, D), BF), ((z.ny, z.pr, D), F32), ((z.ny, z.lr, D), F32), ((L, z.rq, z.inner), F32),
        ((L, z.rq, 2 * z.inner), F32), ((L, z.ro, D), F32), ((L, z.rq, z.ff), F32), ((L, z.rd, D), F32),
        ((L, 6, width), F32),
    ]
    return pl.pallas_call(
        functools.partial(finish_kernel, z),
        grid=(L,),
        out_shape=[jax.ShapeDtypeStruct(s, d) for s, d in outs],
        in_specs=[
            step(z.lr, D), step(z.pr, D), step(z.lr, D), step(3, 2, z.rq, z.half), step(2, 2, z.ro, z.quart),
            step(z.chips, z.rq, z.fs), step(z.dp, z.rd, D), whole(z.chips, 16, z.lanes),
        ],
        out_specs=[step(*s[1:]) for s, _ in outs[:-1]] + [whole(L, 6, width)],
        compiler_params=pltpu.CompilerParams(vmem_limit_bytes=62 * 2**20),
    )(o.lat_out, o.gmedia_out, o.glat_out, o.qs_out, o.os_out, o.upr, o.dnr, o.gnr)


def body(mesh, media, latents, counts, wq, wkv, wout, wup, wdown, norms, cotangent):
    z = Sizes(mesh, media, latents, wq, wkv, wout, wup, wdown)
    L, D, H = z.layers, z.d, z.half
    i, s = lax.axis_index("img"), lax.axis_index("seq")
    y, c = s // 2, s % 2
    k = i * z.ny + y
    pos = k % TP
    media, latents, cotangent = media.astype(z.mt), latents.astype(z.lt), cotangent.astype(z.lt)
    own = norms.reshape(6 * L, -1)
    if z.fused:
        width = own.shape[1]
        tile = jnp.zeros((16, z.lanes), own.dtype)
        tile = lax.dynamic_update_slice(tile, own, (0, s * width))
        o = call(z, media, latents, cotangent, counts, tile, wq, wkv, wout, wup, wdown)
        return tuple(finish(z, o))

    def pick(v, axis, index):
        return lax.dynamic_index_in_dim(v, index, axis, keepdims=False)

    def gather(v, axis):
        return lax.all_gather(v, BOTH, axis=axis, tiled=True)

    nrm = jnp.pad(gather(own, 1).astype(F32), ((0, 16 - 6 * L), (0, 0)))
    fq = pick(gather(wq, 1).reshape(L, D, 2, H), 2, c)
    fkv = pick(gather(wkv, 1).reshape(L, D, 2, 2, H), 3, c).reshape(L, D, 2 * H)
    fq = fq.reshape(L, *z.blk, z.qrows, H)
    fk, fv = (fkv[:, :, n * H:(n + 1) * H].reshape(L, *z.blk, z.qrows, H) for n in range(2))
    wo = gather(wout, 1).reshape(L, *z.blk, 2, z.orows // 2, D)
    fup = pick(gather(wup, 1).reshape(L, D, z.dp, TP, z.fc), 3, pos).reshape(L, 1, 2, D // 2, z.fs)
    fdn = pick(gather(wdown, 1).reshape(L, z.dp, TP, z.fc, D), 2, pos).reshape(L, 1, 2, z.fs // 2, D)
    o = call(z, media, latents, cotangent, counts, nrm, fq, fk, fv, wo, fup, fdn)

    def spread(g, shape, axis, index):
        return lax.dynamic_update_index_in_dim(jnp.zeros(shape, F32), g.astype(F32), index, axis)

    def scatter(g):
        return lax.psum_scatter(g, BOTH, scatter_dimension=1, tiled=True)

    gao = o.gao_out.reshape(L, z.nblk, 2, z.orows, z.quart)
    gout = jnp.concatenate([gao[:, :, 0], gao[:, :, 1]], axis=3).reshape(L, z.inner, D // 2)
    gat = jnp.concatenate([v.reshape(L, D, H) for v in (o.gaq_out, o.gak_out, o.gav_out)], axis=2)
    gq = scatter(spread(gat[:, :, :H], (L, D, 2, H), 2, c).reshape(L, D, z.inner))
    gkv = spread(gat[:, :, H : 3 * H].reshape(L, D, 2, H), (L, D, 2, 2, H), 3, c)
    gkv = scatter(gkv.reshape(L, D, 2 * z.inner))
    go = scatter(spread(gout, (L, z.inner, 2, D // 2), 2, c).reshape(L, z.inner, D))
    gu = spread(o.gup_out.reshape(L, D, z.dp, z.fc), (L, D, z.dp, TP, z.fc), 3, pos)
    gu = scatter(gu.reshape(L, D, z.ff))
    gd = spread(o.gdn_out.reshape(L, z.dp, z.fc, D), (L, z.dp, TP, z.fc, D), 2, pos)
    gd = scatter(gd.reshape(L, z.ff, D))
    gn = lax.psum_scatter(o.gn_out, BOTH, scatter_dimension=1, tiled=True)[: 6 * L].reshape(L, 6, -1)
    return o.lat_out.astype(BF), o.gmedia_out.astype(F32), o.glat_out, gq, gkv, go, gu, gd, gn


def solution(mesh):
    rows = P("img", "seq", None)
    weight = P(None, BOTH, None)
    return jax.shard_map(
        functools.partial(body, mesh),
        mesh=mesh,
        in_specs=(rows, rows, P("img"), weight, weight, weight, weight, weight, P(None, None, BOTH), rows),
        out_specs=(rows, rows, rows, weight, weight, weight, weight, weight, P(None, None, BOTH)),
        check_vma=False,
    )
```

```python
import functools
import types

import jax
import jax.numpy as jnp
from jax import lax
from jax.experimental import pallas as pl
from jax.experimental.pallas import tpu as pltpu
from jax.sharding import PartitionSpec as P

HEAD = 64
EPS = 1e-05
MESH = pl.DeviceIdType.MESH
BF = jnp.bfloat16
F32 = jnp.float32
TP = 8
BOTH = ("img", "seq")


class Sizes:
    def __init__(self, mesh, media, latents, wq, wkv, wout, wup, wdown):
        self.ni, self.ns = mesh.shape["img"], mesh.shape["seq"]
        self.ny = self.ns // 2
        self.chips = self.ni * self.ny
        self.layers = wq.shape[0]
        self.d = media.shape[2]
        self.nimg, self.pr = media.shape[0], media.shape[1]
        self.lr = latents.shape[1]
        self.inner = wq.shape[2]
        self.half = self.inner // 2
        self.ff = wup.shape[2]
        self.fs = self.ff // TP
        self.dp = self.chips // TP
        self.fc = self.ff // self.chips
        self.pm = self.pr * self.ns
        self.latn = self.lr * self.ns
        self.r = self.latn // 2
        self.keys = self.pm + self.latn
        self.heads = self.half // HEAD
        self.rows = TP * self.r
        self.mt = BF if self.pr % 16 == 0 else F32
        self.lt = BF if self.lr % 16 == 0 else F32
        self.rq, self.ro, self.rd = wq.shape[1], wout.shape[1], wdown.shape[1]
        self.lanes = self.d // self.ni
        whole_tiles = all(v % 16 == 0 for v in (self.rq, self.ro, self.rd))
        whole_tiles = whole_tiles and self.fc % 128 == 0 and self.lanes % 128 == 0
        self.fused = whole_tiles and self.ny == 2 == self.layers and self.ni % 4 == 0
        self.blk = (self.ni // 2, 2, self.ny) if self.fused else (2, 1, 1)
        self.nblk = self.blk[0] * self.blk[1] * self.blk[2]
        self.qrows = self.d // self.nblk
        self.orows = self.inner // self.nblk
        self.quart = self.d // 4
        assert self.nimg == self.ny and TP % self.ny == 0


def dot(a, b, ca=1, cb=0):
    return lax.dot_general(a, b, (((ca,), (cb,)), ((), ())), preferred_element_type=F32)


def centre(v):
    c = v - jnp.mean(v, axis=-1, keepdims=True)
    rstd = lax.rsqrt(jnp.mean(c * c, axis=-1, keepdims=True) + EPS)
    return c * rstd, rstd


def pull(xhat, rstd, cot, gain):
    g = cot * gain
    m1 = jnp.mean(g, axis=-1, keepdims=True)
    m2 = jnp.mean(g * xhat, axis=-1, keepdims=True)
    return rstd * (g - m1 - xhat * m2)


def col_sum(v):
    return jnp.sum(v, axis=0, keepdims=True)


def inputs_of(z):
    names = ["media_in", "lat_in", "cot_in", "counts", "nrm_in"]
    if z.fused:
        names += ["wq_in", "wkv_in", "wo_in", "wup_in", "wdn_in"]
    else:
        names += ["wq_in", "wk_in", "wv_in", "wo_in", "wup_in", "wdn_in"]
    return [(n, pltpu.SMEM if n == "counts" else pl.ANY) for n in names]


def outputs_of(z):
    L, D = z.layers, z.d
    outs = dict(
        lat_out=((z.ny, z.lr, D), z.lt),
        gmedia_out=((z.ny, z.pr, D), z.mt),
        glat_out=((z.ny, z.lr, D), F32),
    )
    if z.fused:
        outs.update(
            qs_out=((L, 3, 2, z.rq, z.half), F32),
            os_out=((L, 2, 2, z.ro, z.quart), F32),
            upr=((L, z.chips, z.rq, z.fs), BF),
            dnr=((L, z.dp, z.rd, D), BF),
            gnr=((z.chips, 16, z.lanes), F32),
        )
    else:
        outs.update(
            gaq_out=((L, *z.blk, z.qrows, z.half), BF),
            gak_out=((L, *z.blk, z.qrows, z.half), BF),
            gav_out=((L, *z.blk, z.qrows, z.half), BF),
            gao_out=((L, *z.blk, 2 * z.orows, z.quart), BF),
            gup_out=((L, 1, 2, D // 2, z.fs), BF),
            gdn_out=((L, 1, 2, z.fs // 2, D), BF),
            gn_out=((16, D), F32),
        )
    return outs


def scratch_of(z):
    L, D, R, T = z.layers, z.d, z.r, TP
    kq = z.heads * z.latn
    cu = z.chips if z.fused else 1
    gd = z.dp if z.fused else 1
    v = dict(
        media=((z.ns, z.pr, D), z.mt),
        lc=((2, z.ny, z.lr, D), z.lt),
        mn=((L, z.keys, D), BF),
        kv=((L, z.keys, 2 * z.half), BF),
        wq=((L, *z.blk, z.qrows, z.half), BF),
        wk=((L, *z.blk, z.qrows, z.half), BF),
        wv=((L, *z.blk, z.qrows, z.half), BF),
        wo=((L, *z.blk, 2, z.orows // 2, D), BF),
        wup=((L, cu, 2, D // (2 * cu), z.fs), BF),
        wdn=((L, gd, 2, z.fs // (2 * gd), D), BF),
        nrm=((16, D), F32),
        q4=((L, kq, z.half), BF),
        pexp=((L, kq, z.keys), F32),
        rtot=((L, kq, 1), F32),
        att4=((L, z.latn, z.half), F32),
        atta=((L, 2, z.latn, z.half), BF),
        aft=((L, R, D), F32),
        ffa=((L, T, R, D), BF),
        hp=((L, z.rows, z.fs), F32),
        act=((L, z.rows, z.fs), BF),
        xs=((L, R, D), F32),
        gza=((L, T, R, D), BF),
        psend=((2 * L, T, R, D), BF),
        precv=((2 * L, T, R, D), BF),
        gpre=((L, z.rows, z.fs), BF),
        gya=((L, 2, R, D), BF),
        gl=((L, 2, R, D), F32),
        grecv=((L, R, D), F32),
        gkvm=((L, z.keys, 2 * z.half), BF),
        macc=((z.pm, D), F32),
        msend=((z.pm // 2, D), z.mt),
        mrecv=((z.pm // 2, D), z.mt),
        gn=((16, D), F32),
        xout=((z.ny, z.lr, D), z.lt),
        gxo=((z.ny, z.lr, D), F32),
        cm=((z.pm, D), F32),
        fold=((kq, z.half), F32),
        gak=((L, *z.blk, z.qrows, z.half), BF),
        gav=((L, *z.blk, z.qrows, z.half), BF),
        gaq=((L, *z.blk, z.qrows, z.half), BF),
        gao=((L, *z.blk, 2 * z.orows, z.quart), BF),
        gup=((L, cu, 2, D // (2 * cu), z.fs), BF),
        gdn=((L, gd, 2, z.fs // (2 * gd), D), BF),
    )
    if z.fused:
        za = z.blk[0]
        v.update(
            ntile=((16, z.lanes), BF),
            npair=((16, z.lanes), BF),
            nrecv=((z.chips, 16, z.lanes), BF),
            updr=((L, z.chips, z.rq, z.fs), BF),
            ups=((L, z.chips, z.rq, z.fs), BF),
            dndr=((L, z.dp, z.rd, D), BF),
            dns=((L, z.dp, z.rd, D), BF),
            gns=((16, D), F32),
            gnd=((16, D), F32),
        )
        for part in "kvqo":
            rows, cols = (2 * z.orows, z.quart) if part == "o" else (z.qrows, z.half)
            v["ra" + part] = ((L, za, 2, rows, cols), BF)
            v["sa" + part] = ((L, za, 2, rows, cols), BF)
            v["rb" + part] = ((L, za, rows, cols), BF)
            v["sb" + part] = ((L, za, rows, cols), BF)
            v["rc" + part] = ((L, za, rows, cols), BF)
            v["sf" + part] = ((L, rows, cols), F32)
    out = {n: pltpu.VMEM(s, d) for n, (s, d) in v.items()}
    out.update(ss=pltpu.SemaphoreType.DMA((NSEM,)), rs=pltpu.SemaphoreType.DMA((NSEM,)), ls=pltpu.SemaphoreType.DMA((32,)))
    return out


NSEM = 160


def kernel(z, names, *refs):
    L = z.layers
    q = types.SimpleNamespace(**dict(zip(names, refs)))
    ss, rs, ls = q.ss, q.rs, q.ls
    i = lax.axis_index("img")
    s = lax.axis_index("seq")
    y, c = s // 2, s % 2
    k = i * z.ny + y
    pos, grp = k % TP, k // TP
    sib = (i, y * 2 + (1 - c))
    a, b = i // 2, i % 2

    def chip(kk, cc):
        return (kk // z.ny, (kk % z.ny) * 2 + cc)

    def peer(t):
        return chip(grp * TP + (pos + t) % TP, c)

    waits = []
    used = [0]

    def sem():
        used[0] += 1
        return used[0] - 1

    def send(src, dst, dev, n):
        pltpu.make_async_remote_copy(src, dst, ss.at[n], rs.at[n], device_id=dev, device_id_type=MESH).start()

    def send_by_core(src0, dst0, src1, dst1, dev, n):
        @pl.when(c == 0)
        def _():
            send(src0, dst0, dev, n)

        @pl.when(c == 1)
        def _():
            send(src1, dst1, dev, n)

    def keep(src, dst, n):
        pltpu.make_async_copy(src, dst, rs.at[n]).start()

    def arrive(ref, n):
        pltpu.make_async_copy(ref, ref, rs.at[n]).wait()

    def gone(ref, n):
        pltpu.make_async_copy(ref, ref, ss.at[n]).wait()

    def sent(ref, n):
        waits.append((ref, n))

    bar = pltpu.get_barrier_semaphore()

    def greet(dev):
        pl.semaphore_signal(bar, inc=1, device_id=dev, device_id_type=MESH)

    def greet_chip(t, _):
        greet(chip((k + t) % z.chips, c))
        return 0

    greet(sib)
    for t in range(1, z.ny):
        greet((i, ((y + t) % z.ny) * 2 + (1 - c)))
    lax.fori_loop(1, z.chips, greet_chip, 0)
    pl.semaphore_wait(bar, z.chips - 1 + z.ny)

    def lanes(start, size):
        return pl.ds(pl.multiple_of(start, 128), size)

    def at16(start, size):
        return pl.ds(pl.multiple_of(start, 16), size)

    H = z.half
    if z.fused:
        za = z.blk[0]
        n_w0, n_w1, n_w2, n_w3 = ({p: [sem() for _ in range(L)] for p in "kvqo"} for _ in range(4))
        n_od = [sem() for _ in range(L)]
        n_ua, n_ub, n_da, n_db = ([sem() for _ in range(L)] for _ in range(4))
        n_np, n_nrm = sem(), sem()
        xdev = (i + 1 - 2 * b, s)
        ydev = (i, (1 - y) * 2 + c)
        first = (xdev[0] * (1 - c) + i * c, s * (1 - c) + ydev[1] * c)
        second = (i * (1 - c) + xdev[0] * c, ydev[1] * (1 - c) + s * c)
        bufs = dict(k=q.wk, v=q.wv, q=q.wq)

        def block(p, l, *at):
            if p == "o":
                return q.wo.at[(l, *at, *(slice(None),) * (3 - len(at)), c)]
            return bufs[p].at[(l, *at)]

        def weights_pair(l):
            rows = at16(c * z.rq, z.rq)
            for cc, dev in ((1 - c, sib), (c, None)):
                for p, src in (
                    ("k", q.wkv_in.at[l, :, lanes(cc * H, H)]),
                    ("v", q.wkv_in.at[l, :, lanes(z.inner + cc * H, H)]),
                    ("q", q.wq_in.at[l, :, lanes(cc * H, H)]),
                ):
                    dst = bufs[p].at[l, a, b, y, rows]
                    if dev is None:
                        keep(src, dst, n_w0[p][l])
                    else:
                        send(src, dst, dev, n_w0[p][l])
            for p in "kvq":
                sent(q.wq.at[l, 0, 0, 0, pl.ds(0, z.rq)], n_w0[p][l])
            keep(q.wo_in.at[l], q.wo.at[l, a, b, y, c], n_w0["o"][l])

        def weights_z(l, parts):
            for p in parts:
                own = block(p, l, a, b, y)
                arrive(own, n_w0[p][l])
                for t in range(1, za):
                    send(own, own, (((a + t) % za) * 2 + b, s), n_w1[p][l])

        def weights_first(l, parts):
            for p in parts:
                got = block(p, l, pl.ds(0, za - 1), 0, 0)
                arrive(got, n_w1[p][l])
                sent(got, n_w1[p][l])
                own = block(p, l, slice(None), b, y)
                send(own, own, first, n_w2[p][l])

        def weights_second(l, parts):
            for p in parts:
                got = block(p, l, slice(None), 0, 0)
                arrive(got, n_w2[p][l])
                sent(got, n_w2[p][l])
                ref0, ref1 = block(p, l, slice(None), slice(None), y), block(p, l, slice(None), b)
                send_by_core(ref0, ref0, ref1, ref1, second, n_w3[p][l])

        def weights_end(l, parts):
            for p in parts:
                got = block(p, l, slice(None), 0)
                arrive(got, n_w3[p][l])
                sent(got, n_w3[p][l])
                if p == "o":
                    ref = block(p, l)
                    send(ref, ref, sib, n_od[l])

        def weights_out_end(l):
            ref = q.wo.at[l, :, :, :, 0]
            arrive(ref, n_od[l])
            sent(ref, n_od[l])

        def weights_ff(l):
            def one(t, _):
                kk = (k + t) % z.chips
                dev = chip(kk, c)
                for g in range(z.dp):
                    src = q.wup_in.at[l, :, lanes((g * TP + kk % TP) * z.fc, z.fc)]
                    send(src, q.wup.at[l, k, c, :, pl.ds(g * z.fc, z.fc)], dev, n_ua[l])
                return 0

            for g in range(1, z.dp):
                dev = chip(((grp + g) % z.dp) * TP + pos, c)
                send(q.wdn_in.at[l], q.wdn.at[l, grp, c], dev, n_da[l])
            keep(q.wdn_in.at[l], q.wdn.at[l, grp, c], n_da[l])
            lax.fori_loop(1, z.chips, one, 0)
            for g in range(z.dp):
                src = q.wup_in.at[l, :, lanes((g * TP + pos) * z.fc, z.fc)]
                keep(src, q.wup.at[l, k, c, :, pl.ds(g * z.fc, z.fc)], n_ua[l])
            sent(q.wup.at[l, pl.ds(0, z.chips - 1), 0], n_ua[l])
            sent(q.wdn.at[l, pl.ds(0, z.dp - 1), 0], n_da[l])

        def weights_ff_share(l):
            arrive(q.wup.at[l, :, 0], n_ua[l])
            send(q.wup.at[l, :, c], q.wup.at[l, :, c], sib, n_ub[l])
            arrive(q.wdn.at[l, :, 0], n_da[l])
            send(q.wdn.at[l, :, c], q.wdn.at[l, :, c], sib, n_db[l])

        def weights_ff_end(l):
            arrive(q.wup.at[l, :, 0], n_ub[l])
            sent(q.wup.at[l, :, 0], n_ub[l])
            arrive(q.wdn.at[l, :, 0], n_db[l])
            sent(q.wdn.at[l, :, 0], n_db[l])

        def norms_start():
            send(q.nrm_in, q.ntile, sib, n_np)
            pltpu.make_async_copy(q.nrm_in, q.npair, ls.at[0]).start()

        def norms_spread_in():
            pltpu.make_async_copy(q.nrm_in, q.npair, ls.at[0]).wait()
            arrive(q.ntile, n_np)
            sent(q.ntile, n_np)
            q.nrecv[k] = q.npair[...] + q.ntile[...]

            def one(t, _):
                send(q.nrecv.at[k], q.nrecv.at[k], chip((k + t) % z.chips, c), n_nrm)
                return 0

            lax.fori_loop(1, z.chips, one, 0)

        def norms_end():
            part = q.nrecv.at[pl.ds(0, z.chips - 1)]
            arrive(part, n_nrm)
            sent(part, n_nrm)
            for ii in range(z.ni):
                v = q.nrecv[ii * z.ny].astype(F32)
                for j in range(1, z.ny):
                    v = v + q.nrecv[ii * z.ny + j].astype(F32)
                q.nrm[:, ii * z.lanes:(ii + 1) * z.lanes] = v
    else:
        loads = [(q.nrm_in, q.nrm)]
        for l in range(L):
            loads += [(getattr(q, n + "_in").at[l], getattr(q, n).at[l]) for n in ("wk", "wq", "wo", "wup", "wdn", "wv")]

        def norms_start():
            for n, (src, dst) in enumerate(loads):
                pltpu.make_async_copy(src, dst, ls.at[n]).start()

        def load_end(n):
            pltpu.make_async_copy(*loads[n], ls.at[n]).wait()

        def norms_spread_in():
            pass

        def norms_end():
            load_end(0)

        def nothing(l, parts=None):
            pass

        weights_pair = weights_z = weights_first = weights_second = nothing
        weights_ff = weights_ff_share = nothing

        def weights_end(l, parts):
            for p in parts:
                if p != "o":
                    load_end(1 + 6 * l + dict(k=0, q=1, v=5)[p])

        def weights_out_end(l):
            load_end(3 + 6 * l)

        def weights_ff_end(l):
            load_end(4 + 6 * l)
            load_end(5 + 6 * l)

    def w_q(l):
        return q.wq[l].reshape(z.d, H)

    def w_k(l):
        return q.wk[l].reshape(z.d, H)

    def w_v(l):
        return q.wv[l].reshape(z.d, H)

    def w_up(l):
        return q.wup[l].reshape(z.d, z.fs)

    def w_dn(l):
        return q.wdn[l].reshape(z.fs, z.d)

    n_la, n_lb, n_ma, n_mb = sem(), sem(), sem(), sem()
    n_ff, n_gz, n_ln, n_at, n_gy, n_gl = ([sem() for _ in range(L)] for _ in range(6))
    n_rs = [sem() for _ in range(2 * L)]
    n_md, n_lo, n_go, n_mo = sem(), sem(), sem(), sem()
    own_slot = s % z.ny

    def rows_start():
        for t in range(1, z.ny):
            yy = (y + t) % z.ny
            send(q.media_in.at[yy], q.media.at[s], (i, yy * 2 + c), n_ma)
        keep(q.media_in.at[y], q.media.at[s], n_ma)
        send(q.media_in.at[y], q.media.at[s], sib, n_mb)
        for yy in range(z.ny):
            to = yy * 2 + s // z.ny

            @pl.when(to != s)
            def _():
                send(q.lat_in.at[yy], q.lc.at[0, own_slot], (i, to), n_la)
                send(q.cot_in.at[yy], q.lc.at[1, own_slot], (i, to), n_lb)

            @pl.when(to == s)
            def _():
                keep(q.lat_in.at[yy], q.lc.at[0, own_slot], n_la)
                keep(q.cot_in.at[yy], q.lc.at[1, own_slot], n_lb)

    def media_share():
        arrive(q.media.at[pl.ds(0, z.ny)], n_ma)
        for t in range(1, z.ny):
            yy = (y + t) % z.ny
            send(q.media.at[yy * 2 + c], q.media.at[yy * 2 + c], sib, n_mb)

    def rows_sent():
        for yy in range(z.ny):
            @pl.when(yy * 2 + s // z.ny != s)
            def _():
                gone(q.lc.at[0, 0], n_la)
                gone(q.lc.at[0, 0], n_lb)
        if z.ny > 1:
            gone(q.media.at[pl.ds(0, z.ny - 1)], n_ma)
        gone(q.media.at[pl.ds(0, z.ny)], n_mb)

    def gather_start(buf, value, n):
        buf[pos] = value
        for t in [3, 5, 6, 7, 1, 2, 4]:
            send(buf.at[pos], buf.at[pos], peer(t), n)

    def gather_end(buf, n):
        arrive(buf.at[pl.ds(0, TP - 1)], n)
        sent(buf.at[pl.ds(0, TP - 1)], n)

    def swap(ref, value, n):
        ref[...] = value
        send(ref, ref, sib, n)
        arrive(ref, n)
        sent(ref, n)

    def scatter_put(part, j):
        q.psend[j] = part.astype(BF).reshape(TP, z.r, z.d)

    def scatter_start(j):
        for t in [3, 5, 6, 7, 1, 2, 4]:
            o = (pos + t) % TP
            send(q.psend.at[j, o], q.precv.at[j, pos], peer(t), n_rs[j])
        q.precv[j, pos] = q.psend[j, pos]

    def scatter_end(j):
        arrive(q.precv.at[j, pl.ds(0, TP - 1)], n_rs[j])
        sent(q.precv.at[j, pl.ds(0, TP - 1)], n_rs[j])
        out = q.precv[j, 0].astype(F32)
        for t in range(1, TP):
            out = out + q.precv[j, t].astype(F32)
        return out

    def vec(l, m):
        return q.nrm[6 * l + m][None, :]

    lane_head = lax.broadcasted_iota(jnp.int32, (1, H), 1) // HEAD

    def stack_heads(v):
        return jnp.concatenate([jnp.where(lane_head == h, v, jnp.zeros_like(v)) for h in range(z.heads)], axis=0)

    def fold_heads(v):
        out = None
        q.fold[...] = v
        for h in range(z.heads):
            part = jnp.where(lane_head == h, q.fold[h * z.latn:(h + 1) * z.latn], 0.0)
            out = part if out is None else out + part
        return out

    key_pos = lax.broadcasted_iota(jnp.int32, (1, z.keys), 1)
    live = (key_pos < q.counts[y]) | (key_pos >= z.pm)

    def norm_piece(j, _):
        xhat, _ = centre(q.media[j].astype(F32))
        rows = pl.ds(pl.multiple_of(j * z.pr, 8), z.pr)
        for l in range(L):
            q.mn[l, rows] = (xhat * vec(l, 0) + vec(l, 1)).astype(BF)
        return 0

    def media_kv(l):
        weights_end(l, "k")
        q.kv[l, :z.pm, :H] = dot(q.mn[l, :z.pm], w_k(l)).astype(BF)
        weights_end(l, "v")
        q.kv[l, :z.pm, H:] = dot(q.mn[l, :z.pm], w_v(l)).astype(BF)

    def attention(l):
        xhat, _ = centre(q.xs[l])
        swap(q.mn.at[l, at16(z.pm + c * z.r, z.r)], (xhat * vec(l, 2) + vec(l, 3)).astype(BF), n_ln[l])
        q.kv[l, z.pm:, :H] = dot(q.mn[l, z.pm:], w_k(l)).astype(BF)
        q.kv[l, z.pm:, H:] = dot(q.mn[l, z.pm:], w_v(l)).astype(BF)
        weights_end(l, "q")
        queries = stack_heads(dot(q.mn[l, z.pm:], w_q(l)).astype(BF))
        q.q4[l] = queries
        scores = dot(queries, q.kv[l, :, :H], 1, 1) * 0.125
        scores = jnp.where(live, scores, -1000000000.0)
        e = jnp.exp(scores - jnp.max(scores, axis=-1, keepdims=True))
        rt = jnp.sum(e, axis=-1, keepdims=True)
        q.pexp[l] = e
        q.rtot[l] = rt

    def attention_mix(l):
        own = fold_heads(dot(q.pexp[l].astype(BF), q.kv[l, :, H:]) / q.rtot[l])
        q.att4[l] = own
        swap(q.atta.at[l, c], own.astype(BF), n_at[l])

    def attention_out(l):
        mine = at16(c * z.r, z.r)
        att = jnp.concatenate([q.atta[l, 0, mine], q.atta[l, 1, mine]], axis=1)
        after = q.xs[l] + dot(att, q.wo[l].reshape(z.inner, z.d))
        q.aft[l] = after
        xhat, _ = centre(after)
        gather_start(q.ffa.at[l], (xhat * vec(l, 4) + vec(l, 5)).astype(BF), n_ff[l])

    def hidden(l):
        h = dot(q.ffa[l].reshape(z.rows, z.d), w_up(l))
        q.hp[l] = h
        q.act[l] = (h * (0.5 * (1.0 + lax.erf(h * 0.7071067811865476)))).astype(BF)

    def down(l):
        scatter_put(dot(q.act[l], w_dn(l)), l)

    def ff_back(l):
        g = dot(q.gza[l].reshape(z.rows, z.d), w_dn(l), 1, 1)
        h = q.hp[l]
        slope = 0.5 * (1.0 + lax.erf(h * 0.7071067811865476)) + h * 0.3989422804014327 * jnp.exp(-0.5 * h * h)
        q.gpre[l] = (g * slope).astype(BF)
        scatter_put(dot(q.gpre[l], w_up(l), 1, 1), L + l)
        scatter_start(L + l)

    def ff_grads(l):
        q.gdn[l] = dot(q.act[l], q.gza[l].reshape(z.rows, z.d), 0, 0).astype(BF).reshape(q.gdn.shape[1:])
        q.gup[l] = dot(q.ffa[l].reshape(z.rows, z.d), q.gpre[l], 0, 0).astype(BF).reshape(q.gup.shape[1:])

    def attn_back(l, gx):
        gff = scatter_end(L + l)
        xhat, rstd = centre(q.aft[l])
        q.gn[6 * l + 4] = jnp.sum(gff * xhat, axis=0)
        q.gn[6 * l + 5] = jnp.sum(gff, axis=0)
        gafter = gx + pull(xhat, rstd, gff, vec(l, 4))
        swap(q.gya.at[l, c], gafter.astype(BF), n_gy[l])
        out_grads(l)
        grads_first(l, "o")
        return gafter

    def attn_back_end(l, gafter):
        gy = q.gya[l].reshape(z.latn, z.d)
        hb = z.blk[0] // 2
        wo_own = q.wo[l, pl.ds(c * hb, hb)].reshape(H, z.d)
        gatt = dot(gy, wo_own, 1, 1).astype(BF)
        g4 = stack_heads(gatt.astype(F32))
        delta = jnp.sum(g4 * stack_heads(q.att4[l]), axis=-1, keepdims=True)
        rt = q.rtot[l]
        e = q.pexp[l]
        gp = dot(g4.astype(BF), q.kv[l, :, H:], 1, 1)
        gs = (e / rt * (gp - delta)).astype(BF)
        gq = (fold_heads(dot(gs, q.kv[l, :, :H])) * 0.125).astype(BF)
        gk = (dot(gs, q.q4[l], 0, 0) * 0.125).astype(BF)
        gv = dot(e.astype(BF), (g4 / rt).astype(BF), 0, 0).astype(BF)
        glat = jnp.concatenate([gq, gk[z.pm:], gv[z.pm:]], axis=1)
        w = jnp.concatenate([w_q(l), w_k(l), w_v(l)], axis=1)
        q.gl[l] = dot(glat, w, 1, 1).reshape(2, z.r, z.d)
        send(q.gl.at[l, 1 - c], q.grecv.at[l], sib, n_gl[l])
        q.gkvm[l, :, :H] = gk
        q.gkvm[l, :, H:] = gv
        arrive(q.grecv.at[l], n_gl[l])
        sent(q.grecv.at[l], n_gl[l])
        gln = q.gl[l, c] + q.grecv[l]
        xhat, rstd = centre(q.xs[l])
        q.gn[6 * l + 2] = jnp.sum(gln * xhat, axis=0)
        q.gn[6 * l + 3] = jnp.sum(gln, axis=0)
        return gafter + pull(xhat, rstd, gln, vec(l, 2)), gq

    def out_grads(l):
        att = jnp.concatenate([q.atta[l, 0], q.atta[l, 1]], axis=1)
        cols = lanes(c * (z.d // 2), z.d // 2)
        gyc = jnp.concatenate([q.gya[l, 0, :, cols], q.gya[l, 1, :, cols]], axis=0)
        g = dot(att, gyc, 0, 0).astype(BF).reshape(*z.blk, z.orows, z.d // 2)
        q.gao[l, :, :, :, :z.orows] = g[..., :z.quart]
        q.gao[l, :, :, :, z.orows:] = g[..., z.quart:]

    def qkv_grads(l, gq, p):
        shape = (*z.blk, z.qrows, H)
        if p == "q":
            q.gaq[l] = dot(q.mn[l, z.pm:], gq, 0, 0).astype(BF).reshape(shape)
        elif p == "k":
            q.gak[l] = dot(q.mn[l], q.gkvm[l, :, :H], 0, 0).astype(BF).reshape(shape)
        else:
            q.gav[l] = dot(q.mn[l], q.gkvm[l, :, H:], 0, 0).astype(BF).reshape(shape)

    def media_back(l):
        q.cm[...] = dot(q.gkvm[l, :z.pm], jnp.concatenate([w_k(l), w_v(l)], axis=1), 1, 1)

        def piece(j, sums):
            rows = pl.ds(pl.multiple_of(j * z.pr, 8), z.pr)
            xhat, rstd = centre(q.media[j].astype(F32))
            cotm = q.cm[rows]
            add = cotm * vec(l, 0)
            q.macc[rows] = add if l == L - 1 else q.macc[rows] + add
            return sums[0] + col_sum(cotm * xhat), sums[1] + col_sum(cotm)

        zero = jnp.zeros((1, z.d), F32)
        u, v = lax.fori_loop(0, z.ns, piece, (zero, zero))
        q.gn[6 * l + 0] = u[0]
        q.gn[6 * l + 1] = v[0]

    if z.fused:
        n_ra, n_rb, n_rc, n_rf = ({p: [sem() for _ in range(L)] for p in "kvqo"} for _ in range(4))
        n_ud, n_us, n_dd, n_ds = ([sem() for _ in range(L)] for _ in range(4))
        n_nd, n_ns = sem(), sem()

        def add_to(dst, x, w):
            dst[...] = (x[...].astype(F32) + w[...].astype(F32)).astype(BF)

        def at(name, l):
            return getattr(q, name).at[l]

        def grads_first(l, p):
            g, ra = at("ga" + p, l), at("ra" + p, l)
            send_by_core(g.at[:, :, 1 - y], ra, g.at[:, 1 - b], ra, second, n_ra[p][l])

        def grads_second(l, p):
            g, ra, sa, rb = at("ga" + p, l), at("ra" + p, l), at("sa" + p, l), at("rb" + p, l)
            arrive(ra, n_ra[p][l])
            sent(ra, n_ra[p][l])

            @pl.when(c == 0)
            def _():
                add_to(sa, g.at[:, :, y], ra)

            @pl.when(c == 1)
            def _():
                add_to(sa, g.at[:, b], ra)

            send_by_core(sa.at[:, 1 - b], rb, sa.at[:, 1 - y], rb, first, n_rb[p][l])

        def grads_third(l, p):
            sa, rb, sb, rc = at("sa" + p, l), at("rb" + p, l), at("sb" + p, l), at("rc" + p, l)
            arrive(rb, n_rb[p][l])
            sent(rb, n_rb[p][l])
            add_to(sb, sa.at[:, b * (1 - c) + y * c], rb)
            for t in range(1, za):
                o = (a + t) % za
                send(sb.at[o], rc.at[a], (o * 2 + b, s), n_rc[p][l])
            rc[a] = sb[a]

        def grads_last(l, p):
            rc, sf = at("rc" + p, l), at("sf" + p, l)
            part = rc.at[pl.ds(0, za - 1)]
            arrive(part, n_rc[p][l])
            sent(part, n_rc[p][l])
            v = rc[0].astype(F32)
            for t in range(1, za):
                v = v + rc[t].astype(F32)
            sf[...] = v
            if p != "o":
                mine, other = sf.at[at16(c * z.rq, z.rq)], sf.at[at16((1 - c) * z.rq, z.rq)]
                out = q.qs_out.at[l, "qkv".index(p), c]
                keep(mine, out, n_rf[p][l])
                send(other, out, sib, n_rf[p][l])
            else:
                for h in range(2):
                    mine, other = (sf.at[at16(h * z.orows + cc * z.ro, z.ro)] for cc in (c, 1 - c))
                    keep(mine, q.os_out.at[l, c, h], n_rf[p][l])
                    send(other, q.os_out.at[l, c, h], sib, n_rf[p][l])

        def grads_out(l, p):
            out = q.os_out.at[l] if p == "o" else q.qs_out.at[l, "qkv".index(p)]
            arrive(out, n_rf[p][l])
            sent(out.at[0], n_rf[p][l])

        def ff_pair(l):
            send(q.gup.at[l, :, 1 - c], q.updr.at[l], sib, n_ud[l])
            send(q.gdn.at[l, :, 1 - c], q.dndr.at[l], sib, n_dd[l])

        def ff_spread(l):
            arrive(q.dndr.at[l], n_dd[l])
            sent(q.dndr.at[l], n_dd[l])
            add_to(q.dns.at[l], q.gdn.at[l, :, c], q.dndr.at[l])
            for g in range(1, z.dp):
                o = (grp + g) % z.dp
                send(q.dns.at[l, o], q.dnr.at[l, grp], chip(o * TP + pos, c), n_ds[l])
            arrive(q.updr.at[l], n_ud[l])
            sent(q.updr.at[l], n_ud[l])
            add_to(q.ups.at[l], q.gup.at[l, :, c], q.updr.at[l])

            def one(t, _):
                kk = (k + t) % z.chips
                send(q.ups.at[l, kk], q.upr.at[l, k], chip(kk, c), n_us[l])
                return 0

            lax.fori_loop(1, z.chips, one, 0)
            keep(q.dns.at[l, grp], q.dnr.at[l, grp], n_ds[l])
            keep(q.ups.at[l, k], q.upr.at[l, k], n_us[l])

        def ff_out(l):
            arrive(q.dnr.at[l], n_ds[l])
            sent(q.dns.at[l, pl.ds(0, z.dp - 1)], n_ds[l])
            arrive(q.upr.at[l], n_us[l])
            sent(q.ups.at[l, pl.ds(0, z.chips - 1)], n_us[l])

        def norms_pair():
            send(q.gn, q.gnd, sib, n_nd)

        def norms_spread():
            arrive(q.gnd, n_nd)
            sent(q.gnd, n_nd)
            q.gns[...] = q.gn[...] + q.gnd[...]

            def one(t, _):
                kk = (k + t) % z.chips
                dev = chip(kk, c)
                send(q.gns.at[:, lanes(dev[0] * z.lanes, z.lanes)], q.gnr.at[k], dev, n_ns)
                return 0

            lax.fori_loop(1, z.chips, one, 0)
            keep(q.gns.at[:, lanes(i * z.lanes, z.lanes)], q.gnr.at[k], n_ns)

        def norms_out():
            arrive(q.gnr, n_ns)
            sent(q.gnr.at[pl.ds(0, z.chips - 1)], n_ns)
    else:
        def grads_first(l, p):
            n = 11 + "kvqo".index(p) * L + l
            pltpu.make_async_copy(getattr(q, "ga" + p).at[l], getattr(q, f"ga{p}_out").at[l], ls.at[n]).start()

        def grads_out(l, p):
            n = 11 + "kvqo".index(p) * L + l
            pltpu.make_async_copy(getattr(q, "ga" + p).at[l], getattr(q, f"ga{p}_out").at[l], ls.at[n]).wait()

        def ff_pair(l):
            pltpu.make_async_copy(q.gup.at[l], q.gup_out.at[l], ls.at[19 + l]).start()
            pltpu.make_async_copy(q.gdn.at[l], q.gdn_out.at[l], ls.at[21 + l]).start()

        def ff_out(l):
            pltpu.make_async_copy(q.gup.at[l], q.gup_out.at[l], ls.at[19 + l]).wait()
            pltpu.make_async_copy(q.gdn.at[l], q.gdn_out.at[l], ls.at[21 + l]).wait()

        grads_second = grads_third = grads_last = ff_spread = nothing

        def norms_pair():
            pass

        def norms_spread():
            pass

        def norms_out():
            pltpu.make_async_copy(q.gn, q.gn_out, ls.at[23]).start()
            pltpu.make_async_copy(q.gn, q.gn_out, ls.at[23]).wait()

    weights_pair(0)
    norms_start()
    rows_start()
    weights_z(0, "k")
    weights_z(0, "v")
    weights_z(0, "q")
    weights_z(0, "o")
    norms_spread_in()
    for l in range(1, L):
        weights_pair(l)
    weights_first(0, "k")
    arrive(q.lc.at[0], n_la)
    q.xs[0] = q.lc[0].astype(F32).reshape(z.r, z.d)
    media_share()
    weights_first(0, "v")
    norms_end()
    weights_second(0, "k")
    weights_first(0, "q")
    arrive(q.media.at[pl.ds(0, z.ny)], n_mb)
    weights_second(0, "v")
    weights_first(0, "o")
    for l in range(1, L):
        weights_z(l, "kvqo")
    lax.fori_loop(0, z.ns // 2, norm_piece, 0)
    weights_second(0, "q")
    weights_ff(0)
    lax.fori_loop(z.ns // 2, z.ns, norm_piece, 0)
    weights_second(0, "o")
    arrive(q.lc.at[1], n_lb)
    cot = q.lc[1].astype(F32).reshape(z.r, z.d)
    media_kv(0)
    for l in range(L):
        attention(l)
        if l + 1 < L:
            weights_first(l + 1, "kvqo")
        else:
            gather_start(q.gza.at[l], cot.astype(BF), n_gz[l])
        weights_end(l, "o")
        attention_mix(l)
        weights_out_end(l)
        attention_out(l)
        if l + 1 < L:
            weights_second(l + 1, "kvqo")
        weights_ff_share(l)
        weights_ff_end(l)
        if l + 1 < L:
            weights_ff(l + 1)
        gather_end(q.ffa.at[l], n_ff[l])
        hidden(l)
        if l + 1 < L:
            down(l)
            scatter_start(l)
            media_kv(l + 1)
            q.xs[l + 1] = q.aft[l] + scatter_end(l)
    gx = cot
    for l in reversed(range(L)):
        if l < L - 1:
            gather_start(q.gza.at[l], gx.astype(BF), n_gz[l])
            qkv_grads(l + 1, gq, "k")
            grads_first(l + 1, "k")
            grads_second(l + 1, "o")
            qkv_grads(l + 1, gq, "v")
            qkv_grads(l + 1, gq, "q")
            media_back(l + 1)
        gather_end(q.gza.at[l], n_gz[l])
        ff_back(l)
        if l < L - 1:
            grads_first(l + 1, "v")
            grads_first(l + 1, "q")
        ff_grads(l)
        ff_pair(l)
        if l < L - 1:
            grads_second(l + 1, "k")
            grads_third(l + 1, "o")
        else:
            down(l)
            scatter_start(l)
        ff_spread(l)
        gafter = attn_back(l, gx)
        if l < L - 1:
            grads_second(l + 1, "v")
            grads_second(l + 1, "q")
            grads_third(l + 1, "k")
        gx, gq = attn_back_end(l, gafter)
    qkv_grads(0, gq, "k")
    grads_first(0, "k")
    qkv_grads(0, gq, "v")
    grads_first(0, "v")
    qkv_grads(0, gq, "q")
    grads_first(0, "q")
    grads_second(0, "o")
    for l in range(1, L):
        grads_third(l, "v")
        grads_third(l, "q")
        grads_last(l, "o")
        grads_last(l, "k")
    q.gxo[...] = gx.reshape(z.ny, z.lr, z.d)
    q.xout[...] = (q.aft[L - 1] + scatter_end(L - 1)).astype(z.lt).reshape(z.ny, z.lr, z.d)

    def give_back(srcs, out, n):
        for j in range(z.ny):
            to = c * z.ny + j

            @pl.when(to != s)
            def _():
                send(srcs[j], out.at[y], (i, to), n)

            @pl.when(to == s)
            def _():
                keep(srcs[j], out.at[y], n)

    give_back([q.xout.at[j] for j in range(z.ny)], q.lat_out, n_lo)
    give_back([q.gxo.at[j] for j in range(z.ny)], q.glat_out, n_go)
    media_back(0)
    norms_pair()
    h = z.pm // 2
    q.msend[...] = q.macc[at16((1 - c) * h, h)].astype(z.mt)
    send(q.msend, q.mrecv, sib, n_md)
    grads_second(0, "k")
    grads_second(0, "v")
    grads_second(0, "q")
    grads_third(0, "o")
    norms_spread()
    arrive(q.mrecv, n_md)
    sent(q.mrecv, n_md)
    xhat, rstd = centre(q.media[pl.ds(c * z.ny, z.ny)].astype(F32).reshape(h, z.d))
    gm = pull(xhat, rstd, q.macc[at16(c * h, h)] + q.mrecv[...].astype(F32), jnp.ones((1, z.d), F32))
    mo = q.mn.at[0] if z.mt == BF else q.cm
    for j in range(z.ny):
        mo[j * z.pr:(j + 1) * z.pr] = gm[j * z.pr:(j + 1) * z.pr].astype(z.mt)
    srcs = [mo.at[pl.ds(j * z.pr, z.pr)] for j in range(z.ny)]
    give_back(srcs, q.gmedia_out, n_mo)
    grads_third(0, "k")
    grads_third(0, "v")
    grads_third(0, "q")
    for l in range(1, L):
        grads_last(l, "v")
        grads_last(l, "q")
    grads_last(0, "o")
    for l in range(1, L):
        grads_out(l, "o")
        grads_out(l, "k")
        grads_out(l, "v")
        grads_out(l, "q")
        ff_out(l)
    ff_out(0)
    norms_out()
    grads_last(0, "k")
    grads_last(0, "v")
    grads_last(0, "q")
    grads_out(0, "o")
    grads_out(0, "k")
    grads_out(0, "v")
    grads_out(0, "q")
    arrive(q.lat_out, n_lo)
    arrive(q.glat_out, n_go)
    arrive(q.gmedia_out, n_mo)
    rows_sent()
    for j in range(z.ny):
        @pl.when(c * z.ny + j != s)
        def _():
            gone(q.xout.at[0], n_lo)
            gone(q.gxo.at[0], n_go)
            gone(srcs[0], n_mo)
    for ref, n in waits:
        gone(ref, n)


def call(z, *args):
    ins, outs, scratch = inputs_of(z), outputs_of(z), scratch_of(z)
    names = [n for n, _ in ins] + list(outs) + list(scratch)
    got = pl.pallas_call(
        functools.partial(kernel, z, names),
        out_shape=[jax.ShapeDtypeStruct(s, d) for s, d in outs.values()],
        in_specs=[pl.BlockSpec(memory_space=m) for _, m in ins],
        out_specs=[pl.BlockSpec(memory_space=pl.ANY)] * len(outs),
        scratch_shapes=list(scratch.values()),
        compiler_params=pltpu.CompilerParams(collective_id=0, has_side_effects=True, vmem_limit_bytes=62 * 2**20),
    )(*args)
    return types.SimpleNamespace(**dict(zip(outs, got)))


def finish_kernel(z, lat_in, gm_in, gl_in, qs, os, upr, dnr, gnr, lat, gm, gl, gq, gkv, go, gup, gdn, gn):
    H = z.half
    lat[...] = lat_in[...]
    gm[...] = gm_in[...].astype(F32)
    gl[...] = gl_in[...]
    for cc in range(2):
        gq[0, :, cc * H:(cc + 1) * H] = qs[0, 0, cc]
        gkv[0, :, cc * H:(cc + 1) * H] = qs[0, 1, cc]
        gkv[0, :, z.inner + cc * H:z.inner + (cc + 1) * H] = qs[0, 2, cc]
        for h in range(2):
            col = cc * (z.d // 2) + h * z.quart
            go[0, :, col:col + z.quart] = os[0, cc, h]
    v = dnr[0, 0].astype(F32)
    for g in range(1, z.dp):
        v = v + dnr[0, g].astype(F32)
    gdn[0] = v
    for p in range(TP):
        v = upr[0, p].astype(F32)
        for g in range(1, z.dp):
            v = v + upr[0, g * TP + p].astype(F32)
        for g in range(z.dp):
            col = (g * TP + p) * z.fc
            gup[0, :, col:col + z.fc] = v[:, g * z.fc:(g + 1) * z.fc]
    s = lax.axis_index("seq")
    width = z.lanes // z.ns
    v = gnr[0]
    for t in range(1, z.chips):
        v = v + gnr[t]
    mine = v[:, :width]
    for j in range(1, z.ns):
        mine = jnp.where(s == j, v[:, j * width:(j + 1) * width], mine)
    for l in range(z.layers):
        gn[l] = mine[6 * l:6 * l + 6]


def finish(z, o):
    L, D = z.layers, z.d
    step = lambda *shape: pl.BlockSpec((1, *shape), lambda n: (n,) + (0,) * len(shape))
    whole = lambda *shape: pl.BlockSpec(shape, lambda n: (0,) * len(shape))
    width = z.lanes // z.ns
    outs = [
        ((z.ny, z.lr, D), BF), ((z.ny, z.pr, D), F32), ((z.ny, z.lr, D), F32), ((L, z.rq, z.inner), F32),
        ((L, z.rq, 2 * z.inner), F32), ((L, z.ro, D), F32), ((L, z.rq, z.ff), F32), ((L, z.rd, D), F32),
        ((L, 6, width), F32),
    ]
    return pl.pallas_call(
        functools.partial(finish_kernel, z),
        grid=(L,),
        out_shape=[jax.ShapeDtypeStruct(s, d) for s, d in outs],
        in_specs=[
            step(z.lr, D), step(z.pr, D), step(z.lr, D), step(3, 2, z.rq, z.half), step(2, 2, z.ro, z.quart),
            step(z.chips, z.rq, z.fs), step(z.dp, z.rd, D), whole(z.chips, 16, z.lanes),
        ],
        out_specs=[step(*s[1:]) for s, _ in outs[:-1]] + [whole(L, 6, width)],
        compiler_params=pltpu.CompilerParams(vmem_limit_bytes=62 * 2**20),
    )(o.lat_out, o.gmedia_out, o.glat_out, o.qs_out, o.os_out, o.upr, o.dnr, o.gnr)


def body(mesh, media, latents, counts, wq, wkv, wout, wup, wdown, norms, cotangent):
    z = Sizes(mesh, media, latents, wq, wkv, wout, wup, wdown)
    L, D, H = z.layers, z.d, z.half
    i, s = lax.axis_index("img"), lax.axis_index("seq")
    y, c = s // 2, s % 2
    k = i * z.ny + y
    pos = k % TP
    media, latents, cotangent = media.astype(z.mt), latents.astype(z.lt), cotangent.astype(z.lt)
    own = norms.reshape(6 * L, -1)
    if z.fused:
        width = own.shape[1]
        tile = jnp.zeros((16, z.lanes), own.dtype)
        tile = lax.dynamic_update_slice(tile, own, (0, s * width))
        o = call(z, media, latents, cotangent, counts, tile, wq, wkv, wout, wup, wdown)
        return tuple(finish(z, o))

    def pick(v, axis, index):
        return lax.dynamic_index_in_dim(v, index, axis, keepdims=False)

    def gather(v, axis):
        return lax.all_gather(v, BOTH, axis=axis, tiled=True)

    nrm = jnp.pad(gather(own, 1).astype(F32), ((0, 16 - 6 * L), (0, 0)))
    fq = pick(gather(wq, 1).reshape(L, D, 2, H), 2, c)
    fkv = pick(gather(wkv, 1).reshape(L, D, 2, 2, H), 3, c).reshape(L, D, 2 * H)
    fq = fq.reshape(L, *z.blk, z.qrows, H)
    fk, fv = (fkv[:, :, n * H:(n + 1) * H].reshape(L, *z.blk, z.qrows, H) for n in range(2))
    wo = gather(wout, 1).reshape(L, *z.blk, 2, z.orows // 2, D)
    fup = pick(gather(wup, 1).reshape(L, D, z.dp, TP, z.fc), 3, pos).reshape(L, 1, 2, D // 2, z.fs)
    fdn = pick(gather(wdown, 1).reshape(L, z.dp, TP, z.fc, D), 2, pos).reshape(L, 1, 2, z.fs // 2, D)
    o = call(z, media, latents, cotangent, counts, nrm, fq, fk, fv, wo, fup, fdn)

    def spread(g, shape, axis, index):
        return lax.dynamic_update_index_in_dim(jnp.zeros(shape, F32), g.astype(F32), index, axis)

    def scatter(g):
        return lax.psum_scatter(g, BOTH, scatter_dimension=1, tiled=True)

    gao = o.gao_out.reshape(L, z.nblk, 2, z.orows, z.quart)
    gout = jnp.concatenate([gao[:, :, 0], gao[:, :, 1]], axis=3).reshape(L, z.inner, D // 2)
    gat = jnp.concatenate([v.reshape(L, D, H) for v in (o.gaq_out, o.gak_out, o.gav_out)], axis=2)
    gq = scatter(spread(gat[:, :, :H], (L, D, 2, H), 2, c).reshape(L, D, z.inner))
    gkv = spread(gat[:, :, H : 3 * H].reshape(L, D, 2, H), (L, D, 2, 2, H), 3, c)
    gkv = scatter(gkv.reshape(L, D, 2 * z.inner))
    go = scatter(spread(gout, (L, z.inner, 2, D // 2), 2, c).reshape(L, z.inner, D))
    gu = spread(o.gup_out.reshape(L, D, z.dp, z.fc), (L, D, z.dp, TP, z.fc), 3, pos)
    gu = scatter(gu.reshape(L, D, z.ff))
    gd = spread(o.gdn_out.reshape(L, z.dp, z.fc, D), (L, z.dp, TP, z.fc, D), 2, pos)
    gd = scatter(gd.reshape(L, z.ff, D))
    gn = lax.psum_scatter(o.gn_out, BOTH, scatter_dimension=1, tiled=True)[: 6 * L].reshape(L, 6, -1)
    return o.lat_out.astype(BF), o.gmedia_out.astype(F32), o.glat_out, gq, gkv, go, gu, gd, gn


def solution(mesh):
    rows = P("img", "seq", None)
    weight = P(None, BOTH, None)
    return jax.shard_map(
        functools.partial(body, mesh),
        mesh=mesh,
        in_specs=(rows, rows, P("img"), weight, weight, weight, weight, weight, P(None, None, BOTH), rows),
        out_specs=(rows, rows, rows, weight, weight, weight, weight, weight, P(None, None, BOTH)),
        check_vma=False,
    )
```
